128 devices in a mesh: row: 8 (over x_lo, y), col: 16 (over x_hi, z, core).
Axes of the slice: x: 4 (x_hi: 2, x_lo: 2; x = x_hi * 2 + x_lo), y: 4, z: 4, core: 2. Of those that a mesh axis runs over, the one named last changes fastest.
Arguments:
- blocks: bfloat16 [8, 16, 24, 256, 256], P('row', 'col'), may hold values from 0.049804688 to 1
- block_rows: int32 [8, 16, 24], P('row', 'col'), may hold values from 0 to 255, as said below
- block_cols: int32 [8, 16, 24], P('row', 'col'), may hold values from 0 to 255
- live_count: int32 [8, 16], P('row', 'col'), may hold values from 6 to 24, as said below
- slab: bfloat16 [65536, 2048], P(('row', 'col')), may hold values from 0.0099487305 to 1
Outputs:
- inflated: float32 [65536, 2048], P(('row', 'col'))
The draws below stay inside these ranges and needn't reach their ends.
Inputs may be any that keep to these rules, and one draw needn't show every extreme that they name: For tile (i, j) the 24 slots name distinct block positions; block_rows lie in i * 32 to (i + 1) * 32 - 1, and block_cols are among the numbers ((c // 2) * 16 + j) * 2 + c % 2 for c in 0 to 15. `live_count`: some tile is full and some tile holds the fewest.
All inputs are finite; a program needn't handle non-finite values.
Results may differ from the reference program's by a relative error of at most 0.0003.
Values may be sent and summed in bfloat16 or wider, within the bound.
A program may use at most 320 MiB of HBM per device.

```python
import math
import jax
import jax.numpy as jnp
from jax import lax

BS = 256
BR_DEV = 2
NNZ = 24
K = 2048
TILE_ROWS = 32
TILE_COLS = 16
PROTEINS = 65536
N_ROW = 8
N_COL = 16


def tile_layout(key):
    row_count = TILE_COLS // BR_DEV
    col_count = TILE_ROWS // BR_DEV
    base = jax.random.fold_in(key, 11)
    keys = jax.random.split(base, row_count * col_count)
    places = jax.vmap(lambda single: jax.random.permutation(single, TILE_ROWS * TILE_COLS)[:NNZ])(keys)
    places = places.reshape(row_count, col_count, NNZ).astype(jnp.int32)
    local_rows = places // TILE_COLS
    local_cols = places % TILE_COLS
    row_group = jnp.arange(row_count, dtype=jnp.int32)[:, None, None]
    col_group = jnp.arange(col_count, dtype=jnp.int32)[None, :, None]
    global_rows = row_group * TILE_ROWS + local_rows
    global_cols = (local_cols // BR_DEV * col_count + col_group) * BR_DEV + local_cols % BR_DEV
    return (global_rows.astype(jnp.int32), global_cols.astype(jnp.int32))


def draw_block_rows(key, part):
    return tile_layout(key)[0]


def draw_block_cols(key, part):
    return tile_layout(key)[1]


def draw_live_count(key, part):
    row_count = TILE_COLS // BR_DEV
    col_count = TILE_ROWS // BR_DEV
    base = jax.random.fold_in(key, 23)
    counts = jax.random.randint(jax.random.fold_in(base, 1), (row_count * col_count,), NNZ // 4, NNZ + 1)
    order = jax.random.permutation(jax.random.fold_in(base, 2), row_count * col_count)
    counts = counts.at[order[0]].set(NNZ)
    counts = counts.at[order[1]].set(NNZ // 4)
    return counts.reshape(row_count, col_count).astype(jnp.int32)


def block_levels(stream_key, shape, cuts, least, high):
    gain = 1.0
    for position, parts in cuts:
        steps = jax.random.uniform(jax.random.fold_in(jax.random.fold_in(stream_key, 6), position), (parts,), jnp.float32, least / len(cuts), high / len(cuts))
        gain = gain * jnp.repeat(jnp.exp(steps), shape[position] // parts).reshape((-1,) + (1,) * (len(shape) - 1 - position))
    return gain


def setup_inputs(seed: int = 0) -> dict:
    splits = jax.random.split(jax.random.key(seed), 6)
    blocks = jnp.clip(0.049804688 + 0.9501953 * jax.random.uniform(splits[0], (N_ROW, N_COL, NNZ, BS, BS), jnp.float32) ** block_levels(splits[0], (N_ROW, N_COL, NNZ, BS, BS), ((0, 8), (1, 16)), -0.2, 0.2), 0.049804688, 1.0).astype(jnp.bfloat16)
    block_rows = draw_block_rows(jax.random.fold_in(splits[5], 71), 0)
    block_cols = draw_block_cols(jax.random.fold_in(splits[5], 71), 0)
    live_count = draw_live_count(jax.random.fold_in(splits[5], 71), 0)
    slab = jnp.clip(jnp.exp(math.log(1.0) - 4.61031033 * jax.random.uniform(splits[4], (PROTEINS, K), jnp.float32) ** block_levels(splits[4], (PROTEINS, K), ((0, 128),), -0.2, 0.2)), 0.0099487305, 1.0).astype(jnp.bfloat16)
    return dict(blocks=blocks, block_rows=block_rows, block_cols=block_cols, live_count=live_count, slab=slab)


def reference(blocks, block_rows, block_cols, live_count, slab):
    row_tiles, col_tiles, slot_total, block_size, _ = blocks.shape
    weights = blocks.reshape(-1, block_size, block_size)
    rows_flat = block_rows.reshape(-1).astype(jnp.int32)
    cols_flat = block_cols.reshape(-1).astype(jnp.int32)
    in_use = (jnp.arange(slot_total)[None, None, :] < live_count[:, :, None]).reshape(-1)

    def step(expanded, record):
        weight, row_block, col_block, alive = record
        piece = lax.dynamic_slice_in_dim(slab, (col_block * block_size).astype(jnp.int32), block_size, 0)
        product = jnp.dot(weight, piece, preferred_element_type=jnp.float32)
        product = jnp.where(alive, product, jnp.zeros_like(product))
        offset = (row_block * block_size).astype(jnp.int32)
        current = lax.dynamic_slice_in_dim(expanded, offset, block_size, 0)
        return lax.dynamic_update_slice_in_dim(expanded, current + product, offset, 0), None

    start_value = jnp.zeros((slab.shape[0], slab.shape[1]), jnp.float32)
    expanded, _ = lax.scan(step, start_value, (weights, rows_flat, cols_flat, in_use))
    square = expanded * expanded
    column_mass = jnp.sum(square, axis=0)
    return PROTEINS * square / column_mass
```

```python
import functools

import jax
import jax.numpy as jnp
from jax import lax
from jax.experimental import pallas as pl
from jax.experimental.pallas import tpu as pltpu
from jax.sharding import PartitionSpec as P

MESH = pl.DeviceIdType.MESH

LANES = 128
SCALE = 2.0**-6

(OWN, CORE, X, YPA, YMA, YPB, YMB, YPC, YMC, YPD, YMD,
 M1P, M1M, M2AP, M2AM, M2BP, M2BM, MX, OUTC, OUTL) = range(20)
KINDS = 20


def encode(x):
    x = x * SCALE
    x3 = x * x * x
    x6 = x3 * x3
    return (x6 * x6).astype(jnp.bfloat16)


def decode(y):
    y = y.astype(jnp.float32)
    root = jnp.exp2(jnp.log(y) * (1.0 / (12.0 * 0.6931471805599453)) + 6.0)
    return jnp.where(y > 0.0, root, 0.0)


def kernel(chunks, slots, tab, keep, blocks, slab, e_out, mass_out,
           a_buf, b_buf, b_cmp, q_buf, s_buf, t_buf,
           m1s, m1r, m2as, m2ar, m2bs, m2br, mxs, mxr, fin, ms, mr, mfin,
           send, recv, a_send, a_recv, mass_send, mass_recv, cmp_sem):
    i = lax.axis_index("row")
    j = lax.axis_index("col")
    y = lax.rem(i, 4)
    yb = i - y
    q = lax.rem(j, 2)
    z = lax.rem(j // 2, 4)
    xh = j // 8
    zb = xh * 8 + q

    def row_y(d):
        return yb + lax.rem(y + d, 4)

    def col_z(d):
        return zb + 2 * lax.rem(z + d, 4)

    def flip(r):
        return lax.rem(r + 4, 8)

    xi = flip(i)
    yp, y2, ym = row_y(1), row_y(2), row_y(3)
    xyp, xy2, xym = flip(yp), flip(y2), flip(ym)
    jc = j + 1 - 2 * q
    jx = lax.rem(j + 8, 16)
    zp, z2, zm = lax.rem(z + 1, 4), lax.rem(z + 2, 4), lax.rem(z + 3, 4)

    dev_core = (i, jc)
    dev_x = (xi, j)
    dev_x2 = (i, jx)
    dev_yp, dev_ym = (yp, j), (ym, j)
    dev_zp, dev_zm = (i, col_z(1)), (i, col_z(3))
    mass_devs = [
        [(xi, j), (i, jx), (xi, jx)],
        [(row_y(d), j) for d in (1, 2, 3)],
        [(i, col_z(d)) for d in (1, 2, 3)],
    ]

    def cols(half, k):
        return pl.ds(pl.multiple_of(half * (chunks * LANES) + k * LANES, LANES), LANES)

    def remote(kind, k, src, dst, dev):
        return pltpu.make_async_remote_copy(
            src_ref=src, dst_ref=dst, send_sem=send.at[kind, k], recv_sem=recv.at[kind, k],
            device_id=dev, device_id_type=MESH)

    def arrived(kind, k, ref, dev):
        remote(kind, k, ref, ref, dev).wait_recv()

    def piece(k, r, first=0, count=4):
        return b_buf.at[k, pl.ds(r * 4 + first, count)]

    def own_copy(k):
        return pltpu.make_async_copy(slab.at[:, :, cols(q, k)], piece(k, i, q * 2, 2), recv.at[OWN, k])

    def core_copy(k):
        return remote(CORE, k, slab.at[:, :, cols(1 - q, k)], piece(k, i, q * 2, 2), dev_core)

    def piece_copy(kind, k, r, dev, first=0, count=4):
        return remote(kind, k, piece(k, r, first, count), piece(k, r, first, count), dev)

    def x_copy(k):
        return piece_copy(X, k, i, dev_x)

    def y_copies(k):
        return [piece_copy(YPA, k, i, dev_yp), piece_copy(YMA, k, i, dev_ym)]

    def yx_copies(k):
        return [piece_copy(YPB, k, xi, dev_yp), piece_copy(YMB, k, xi, dev_ym)]

    def fwd_copies(k):
        return [piece_copy(YPC, k, ym, dev_yp, 0, 2), piece_copy(YMC, k, yp, dev_ym, 2, 2)]

    def fwdx_copies(k):
        return [piece_copy(YPD, k, xym, dev_yp, 0, 2), piece_copy(YMD, k, xyp, dev_ym, 2, 2)]

    def pair_copies(kp, k, src, dst):
        slot = lax.rem(k, 2)
        return [remote(kp, k, src.at[slot, 0], dst.at[k, 0], dev_zp),
                remote(kp + 1, k, src.at[slot, 1], dst.at[k, 1], dev_zm)]

    def m1_copies(k):
        return pair_copies(M1P, k, m1s, m1r)

    def m2a_copies(k):
        return pair_copies(M2AP, k, m2as, m2ar)

    def m2b_copies(k):
        return pair_copies(M2BP, k, m2bs, m2br)

    def mx_copy(k):
        return remote(MX, k, mxs.at[lax.rem(k, 2)], mxr.at[k], dev_x2)

    def outc_copy(k):
        return remote(OUTC, k, fin.at[lax.rem(k, 2), pl.ds((1 - q) * 2, 2)], e_out.at[:, :, cols(q, k)], dev_core)

    def outl_copy(k):
        return pltpu.make_async_copy(fin.at[lax.rem(k, 2), pl.ds(q * 2, 2)], e_out.at[:, :, cols(q, k)], recv.at[OUTL, k])

    def a_local():
        return pltpu.make_async_copy(blocks, a_buf.at[pl.ds(q * slots, slots)], a_recv.at[0])

    def a_remote():
        mine = a_buf.at[pl.ds(q * slots, slots)]
        return pltpu.make_async_remote_copy(
            src_ref=blocks, dst_ref=mine, send_sem=a_send.at[0], recv_sem=a_recv.at[1],
            device_id=dev_core, device_id_type=MESH)

    def start(copies):
        for copy in copies:
            copy.start()

    barrier = pltpu.get_barrier_semaphore()
    others = [dev_core] + mass_devs[0] + mass_devs[1] + mass_devs[2]
    for dev in others:
        pl.semaphore_signal(barrier, inc=1, device_id=dev, device_id_type=MESH)
    pl.semaphore_wait(barrier, len(others))

    def stage_a(k):
        own_copy(k).wait()
        arrived(CORE, k, piece(k, i, (1 - q) * 2, 2), dev_core)
        x_copy(k).start()
        start(y_copies(k))

    def stage_b(k):
        arrived(X, k, piece(k, xi), dev_x)
        start(yx_copies(k))

    def stage_c(k):
        arrived(YPA, k, piece(k, ym), dev_ym)
        arrived(YMA, k, piece(k, yp), dev_yp)
        start(fwd_copies(k))
        arrived(YPB, k, piece(k, xym), dev_ym)
        arrived(YMB, k, piece(k, xyp), dev_yp)
        start(fwdx_copies(k))

    def partial(r):
        return q_buf[tab[4 * slots + r]]

    def compute(k):
        arrived(YPC, k, piece(k, y2, 0, 2), dev_ym)
        arrived(YMC, k, piece(k, y2, 2, 2), dev_yp)
        arrived(YPD, k, piece(k, xy2, 0, 2), dev_ym)
        arrived(YMD, k, piece(k, xy2, 2, 2), dev_yp)
        move = pltpu.make_async_copy(b_buf.at[k], b_cmp, cmp_sem.at[0])
        move.start()
        move.wait()

        def product(p, _):
            q_buf[p + 1] = keep[p] * q_buf[p] + jnp.dot(
                a_buf[tab[p]], b_cmp[tab[2 * slots + p]], preferred_element_type=jnp.float32)
            return 0

        lax.fori_loop(0, 2 * slots, product, 0)

        slot = lax.rem(k, 2)

        @pl.when(k >= 2)
        def _():
            for copy in m1_copies(k - 2) + m2a_copies(k - 2):
                copy.wait_send()

        def pack1(n, _):
            m1s[slot, 0, n] = encode(partial(z2 * 4 + n))
            m1s[slot, 1, n] = encode(partial(16 + z2 * 4 + n))
            return 0

        lax.fori_loop(0, 4, pack1, 0)
        start(m1_copies(k))

        def pack2(n, _):
            m2as[slot, 0, n] = encode(partial(16 + zp * 4 + n))
            m2as[slot, 1, n] = encode(partial(zm * 4 + n))
            return 0

        lax.fori_loop(0, 4, pack2, 0)
        start(m2a_copies(k))

        keep_slot = lax.rem(k, 3)

        def hold(n, _):
            t_buf[0, n] = partial(zp * 4 + n)
            t_buf[1, n] = partial(16 + zm * 4 + n)
            s_buf[keep_slot, 0, n] = partial(z * 4 + n)
            s_buf[keep_slot, 1, n] = partial(16 + z * 4 + n)
            return 0

        lax.fori_loop(0, 4, hold, 0)

    def relay(k):
        slot = lax.rem(k, 2)

        @pl.when(k >= 2)
        def _():
            for copy in m2b_copies(k - 2):
                copy.wait_send()

        arrived(M1P, k, m1r.at[k, 0], dev_zm)
        arrived(M1M, k, m1r.at[k, 1], dev_zp)

        def pack(n, _):
            for d in range(2):
                m2bs[slot, d, n] = encode(t_buf[d, n] + decode(m1r[k, d, n]))
            return 0

        lax.fori_loop(0, 4, pack, 0)
        start(m2b_copies(k))

    def collect(k):
        slot = lax.rem(k, 2)
        keep_slot = lax.rem(k, 3)

        @pl.when(k >= 2)
        def _():
            mx_copy(k - 2).wait_send()

        arrived(M2AP, k, m2ar.at[k, 0], dev_zm)
        arrived(M2AM, k, m2ar.at[k, 1], dev_zp)
        arrived(M2BP, k, m2br.at[k, 0], dev_zm)
        arrived(M2BM, k, m2br.at[k, 1], dev_zp)

        def total(h, n):
            return s_buf[keep_slot, h, n] + (decode(m2br[k, h, n]) + decode(m2ar[k, 1 - h, n]))

        def pack(n, _):
            mxs[slot, n] = encode(total(1 - xh, n))
            return 0

        lax.fori_loop(0, 4, pack, 0)
        mx_copy(k).start()

        def hold(n, _):
            s_buf[keep_slot, xh, n] = total(xh, n)
            return 0

        lax.fori_loop(0, 4, hold, 0)

    lane_row = lax.broadcasted_iota(jnp.int32, (8, LANES), 0)

    def finish(k):
        slot = lax.rem(k, 2)
        keep_slot = lax.rem(k, 3)

        @pl.when(k >= 2)
        def _():
            outc_copy(k - 2).wait_send()
            outl_copy(k - 2).wait()

        arrived(MX, k, mxr.at[k], dev_x2)

        def add(n, acc):
            value = s_buf[keep_slot, xh, n] + decode(mxr[k, n])
            fin[slot, n] = value
            return acc + jnp.sum((value * value).reshape(-1, 8, LANES), axis=0)

        acc = lax.fori_loop(0, 4, add, jnp.zeros((8, LANES), jnp.float32))
        outc_copy(k).start()
        outl_copy(k).start()
        ms[0] = jnp.where(lane_row == k, jnp.sum(acc, axis=0, keepdims=True), ms[0])

    def first(k, _):
        own_copy(k).start()
        core_copy(k).start()
        return 0

    lax.fori_loop(0, 2, first, 0)
    a_local().start()
    a_remote().start()
    lax.fori_loop(2, chunks, first, 0)
    q_buf[0] = jnp.zeros(q_buf.shape[1:], jnp.float32)
    ms[0] = jnp.zeros((8, LANES), jnp.float32)

    stage_a(0)
    stage_b(0)
    stage_a(1)
    a_local().wait()
    pltpu.make_async_remote_copy(
        src_ref=blocks, dst_ref=a_buf.at[pl.ds((1 - q) * slots, slots)], send_sem=a_send.at[0],
        recv_sem=a_recv.at[1], device_id=dev_core, device_id_type=MESH).wait_recv()

    def step(t, _):
        @pl.when(t < chunks)
        def _():
            stage_c(t)

        @pl.when(t + 1 < chunks)
        def _():
            stage_b(t + 1)

        @pl.when(t + 2 < chunks)
        def _():
            stage_a(t + 2)

        @pl.when((t >= 1) & (t - 1 < chunks))
        def _():
            relay(t - 1)

        @pl.when((t >= 2) & (t - 2 < chunks))
        def _():
            collect(t - 2)

        @pl.when(t >= 3)
        def _():
            finish(t - 3)

        @pl.when(t < chunks)
        def _():
            compute(t)

        return 0

    lax.fori_loop(0, chunks + 3, step, 0)

    for stage in range(3):
        copies = []
        for n, dev in enumerate(mass_devs[stage]):
            copies.append(pltpu.make_async_remote_copy(
                src_ref=ms.at[stage], dst_ref=mr.at[stage, n], send_sem=mass_send.at[stage, n],
                recv_sem=mass_recv.at[stage, n], device_id=dev, device_id_type=MESH))
        start(copies)
        for copy in copies:
            copy.wait()
        ms[stage + 1] = (ms[stage] + mr[stage, 0]) + (mr[stage, 1] + mr[stage, 2])
    last = pltpu.make_async_remote_copy(
        src_ref=ms.at[3], dst_ref=mfin, send_sem=mass_send.at[3, 0], recv_sem=mass_recv.at[3, 0],
        device_id=dev_core, device_id_type=MESH)
    last.start()
    last.wait()
    mass_out[q] = ms[3]
    mass_out[1 - q] = mfin[...]

    a_remote().wait_send()

    def drain(k, _):
        core_copy(k).wait_send()
        x_copy(k).wait_send()
        for copy in y_copies(k) + yx_copies(k) + fwd_copies(k) + fwdx_copies(k):
            copy.wait_send()
        arrived(OUTC, k, e_out.at[:, :, cols(1 - q, k)], dev_core)
        return 0

    lax.fori_loop(0, chunks, drain, 0)

    def drain_last(k, _):
        for copy in m1_copies(k) + m2a_copies(k) + m2b_copies(k):
            copy.wait_send()
        mx_copy(k).wait_send()
        outc_copy(k).wait_send()
        outl_copy(k).wait()
        return 0

    lax.fori_loop(chunks - 2, chunks, drain_last, 0)


def tables(block_rows, block_cols, live_count):
    slots = block_rows.shape[-1]
    q = lax.axis_index("col") % 2
    rows = block_rows.reshape(slots) - lax.axis_index("row") * 32
    cols = block_cols.reshape(slots)
    c = cols // 2 // 16 * 2 + cols % 2
    place = c // 2 * 4 + q * 2 + c % 2
    key = jnp.where(jnp.arange(slots) < live_count.reshape(()), rows, 32)
    mine = jnp.stack([key, place])
    other = lax.ppermute(mine, "col", [(n, n + 1 - 2 * (n % 2)) for n in range(16)])
    key = jnp.concatenate([mine[0], other[0]])
    place = jnp.concatenate([mine[1], other[1]])
    number = jnp.arange(2 * slots)
    block = jnp.where(number < slots, q * slots + number, (1 - q) * slots + number - slots)
    before = (key[:, None] < key[None, :]) | ((key[:, None] == key[None, :]) & (number[:, None] < number[None, :]))
    rank = jnp.sum(before, axis=0)
    hit = rank[None, :] == number[:, None]
    block = jnp.sum(jnp.where(hit, block[None, :], 0), axis=1)
    place = jnp.sum(jnp.where(hit, place[None, :], 0), axis=1)
    again = jnp.any((rank[None, :] + 1 == rank[:, None]) & (key[None, :] == key[:, None]), axis=1)
    keep = jnp.any(hit & again[None, :], axis=1).astype(jnp.float32)
    row = jnp.arange(32)
    upto = jnp.sum(key[None, :] <= row[:, None], axis=1)
    last = jnp.where(jnp.any(key[None, :] == row[:, None], axis=1), upto, 0)
    return jnp.concatenate([block, place, last]).astype(jnp.int32), keep


def body(blocks, block_rows, block_cols, live_count, slab):
    slots, bs = blocks.shape[2], blocks.shape[3]
    depth, width = slab.shape
    chunks = width // 2 // LANES
    tab, keep = tables(block_rows, block_cols, live_count)
    f32, bf16 = jnp.float32, jnp.bfloat16
    tile = (bs, LANES)
    vm = pltpu.VMEM
    e, mass = pl.pallas_call(
        functools.partial(kernel, chunks, slots),
        out_shape=(jax.ShapeDtypeStruct((2, bs, width), f32), jax.ShapeDtypeStruct((2, chunks, LANES), f32)),
        in_specs=[pl.BlockSpec(memory_space=pltpu.SMEM), pl.BlockSpec(memory_space=pltpu.SMEM),
                  pl.BlockSpec(memory_space=pl.ANY), pl.BlockSpec(memory_space=pl.ANY)],
        out_specs=(pl.BlockSpec(memory_space=pl.ANY), pl.BlockSpec(memory_space=pltpu.VMEM)),
        scratch_shapes=[
            vm((2 * slots, bs, bs), bf16),
            vm((chunks, 32) + tile, bf16),
            vm((32,) + tile, bf16),
            vm((2 * slots + 1,) + tile, f32),
            vm((3, 2, 4) + tile, f32),
            vm((2, 4) + tile, f32),
            vm((2, 2, 4) + tile, bf16), vm((chunks, 2, 4) + tile, bf16),
            vm((2, 2, 4) + tile, bf16), vm((chunks, 2, 4) + tile, bf16),
            vm((2, 2, 4) + tile, bf16), vm((chunks, 2, 4) + tile, bf16),
            vm((2, 4) + tile, bf16), vm((chunks, 4) + tile, bf16),
            vm((2, 4) + tile, f32),
            vm((4, chunks, LANES), f32), vm((3, 3, chunks, LANES), f32), vm((chunks, LANES), f32),
            pltpu.SemaphoreType.DMA((KINDS, chunks)), pltpu.SemaphoreType.DMA((KINDS, chunks)),
            pltpu.SemaphoreType.DMA((1,)), pltpu.SemaphoreType.DMA((2,)),
            pltpu.SemaphoreType.DMA((4, 3)), pltpu.SemaphoreType.DMA((4, 3)),
            pltpu.SemaphoreType.DMA((1,)),
        ],
        compiler_params=pltpu.CompilerParams(
            collective_id=0, has_side_effects=True, vmem_limit_bytes=58 * 1024 * 1024),
        cost_estimate=pl.CostEstimate(
            flops=2 * 2 * slots * bs * bs * width // 2, bytes_accessed=16 * 2**20, transcendentals=0),
    )(tab, keep, blocks.reshape(slots, bs, bs), slab.reshape(2, bs, width))
    expanded = e.reshape(depth, width)
    proteins = depth * 128
    return proteins * (expanded * expanded) / mass.reshape(width)


def solution(mesh):
    placed = (
        P("row", "col", None, None, None),
        P("row", "col", None),
        P("row", "col", None),
        P("row", "col"),
        P(("row", "col"), None),
    )
    return jax.shard_map(
        body, mesh=mesh, in_specs=placed, out_specs=P(("row", "col"), None), check_vma=False
    )
```

```python
import functools

import jax
import jax.numpy as jnp
from jax import lax
from jax.experimental import pallas as pl
from jax.experimental.pallas import tpu as pltpu
from jax.sharding import PartitionSpec as P

MESH = pl.DeviceIdType.MESH
LOW, HIGH = pl.ds(0, 128), pl.ds(128, 128)

LANES = 128
SCALE = 2.0**-6

(OWN, CORE, X, YPA, YMA, YPB, YMB, YPC, YMC, YPD, YMD,
 M1P, M1M, M2AP, M2AM, M2BP, M2BM, MX, OUTC, OUTL, X1, EAP, EAM, EBP, EBM) = range(25)
KINDS = 25


def encode(x):
    x = x * SCALE
    x3 = x * x * x
    x6 = x3 * x3
    return (x6 * x6).astype(jnp.bfloat16)


def decode(y):
    y = y.astype(jnp.float32)
    root = jnp.exp2(jnp.log(y) * (1.0 / (12.0 * 0.6931471805599453)) + 6.0)
    return jnp.where(y > 0.0, root, 0.0)


def kernel(chunks, slots, tab, keep, blocks, slab, e_out, mass_out,
           a_buf, b_buf, b_cmp, q_buf, s_buf, t_buf,
           m1s, m1r, m2as, m2ar, m2bs, m2br, mxs, mxr, x1s, x1r, eas, ear, ebs, ebr, u_buf, v_buf,
           fin, ms, mr_plane, mr_line,
           send, recv, a_send, a_recv, mass_send, mass_recv, cmp_sem):
    i = lax.axis_index("row")
    j = lax.axis_index("col")
    y = lax.rem(i, 4)
    yb = i - y
    q = lax.rem(j, 2)
    z = lax.rem(j // 2, 4)
    xh = j // 8
    zb = xh * 8 + q

    def row_y(d):
        return yb + lax.rem(y + d, 4)

    def col_z(d):
        return zb + 2 * lax.rem(z + d, 4)

    def flip(r):
        return lax.rem(r + 4, 8)

    xi = flip(i)
    yp, y2, ym = row_y(1), row_y(2), row_y(3)
    xyp, xy2, xym = flip(yp), flip(y2), flip(ym)
    jc = j + 1 - 2 * q
    jx = lax.rem(j + 8, 16)
    zp, z2, zm = lax.rem(z + 1, 4), lax.rem(z + 2, 4), lax.rem(z + 3, 4)

    dev_core = (i, jc)
    dev_x = (xi, j)
    dev_x2 = (i, jx)
    dev_yp, dev_ym = (yp, j), (ym, j)
    dev_zp, dev_zm = (i, col_z(1)), (i, col_z(3))
    plane = [(lax.rem(yb + 4 * fx, 8) + lax.rem(y + d, 4), lax.rem(j + 8 * fh, 16))
             for fx in range(2) for d in range(4) for fh in range(2)][1:]
    line = [(i, col_z(d)) for d in (1, 2, 3)] + [(i, col_z(d) + 1 - 2 * q) for d in range(4)]

    def cols(half, k):
        return pl.ds(pl.multiple_of(half * (chunks * LANES) + k * LANES, LANES), LANES)

    def remote(kind, k, src, dst, dev):
        return pltpu.make_async_remote_copy(
            src_ref=src, dst_ref=dst, send_sem=send.at[kind, k], recv_sem=recv.at[kind, k],
            device_id=dev, device_id_type=MESH)

    def arrived(kind, k, ref, dev):
        remote(kind, k, ref, ref, dev).wait_recv()

    def piece(k, r, first=0, count=4):
        return b_buf.at[k, pl.ds(r * 4 + first, count)]

    def own_copy(k):
        return pltpu.make_async_copy(slab.at[:, :, cols(q, k)], piece(k, i, q * 2, 2), recv.at[OWN, k])

    def core_copy(k):
        return remote(CORE, k, slab.at[:, :, cols(1 - q, k)], piece(k, i, q * 2, 2), dev_core)

    def piece_copy(kind, k, r, dev, first=0, count=4):
        return remote(kind, k, piece(k, r, first, count), piece(k, r, first, count), dev)

    def x_copy(k):
        return piece_copy(X, k, i, dev_x)

    def y_copies(k):
        return [piece_copy(YPA, k, i, dev_yp), piece_copy(YMA, k, i, dev_ym)]

    def yx_copies(k):
        return [piece_copy(YPB, k, xi, dev_yp), piece_copy(YMB, k, xi, dev_ym)]

    def fwd_copies(k):
        return [piece_copy(YPC, k, ym, dev_yp, 0, 2), piece_copy(YMC, k, yp, dev_ym, 2, 2)]

    def fwdx_copies(k):
        return [piece_copy(YPD, k, xym, dev_yp, 0, 2), piece_copy(YMD, k, xyp, dev_ym, 2, 2)]

    def pair_copies(kp, k, src, dst):
        slot = lax.rem(k, 2)
        return [remote(kp, k, src.at[slot, 0], dst.at[k, 0], dev_zp),
                remote(kp + 1, k, src.at[slot, 1], dst.at[k, 1], dev_zm)]

    def m1_copies(k):
        return pair_copies(M1P, k, m1s, m1r)

    def m2a_copies(k):
        return pair_copies(M2AP, k, m2as, m2ar)

    def m2b_copies(k):
        return pair_copies(M2BP, k, m2bs, m2br)

    def x1_copy(k):
        return remote(X1, k, x1s.at[lax.rem(k, 2)], x1r.at[k], dev_x2)

    def ea_copies(k):
        return pair_copies(EAP, k, eas, ear)

    def eb_copies(k):
        return pair_copies(EBP, k, ebs, ebr)

    def mx_copy(k):
        return remote(MX, k, mxs.at[lax.rem(k, 2)], mxr.at[k], dev_x2)

    def outc_copy(k):
        return remote(OUTC, k, fin.at[lax.rem(k, 2), pl.ds((1 - q) * 2, 2)], e_out.at[:, :, cols(q, k)], dev_core)

    def outl_copy(k):
        return pltpu.make_async_copy(fin.at[lax.rem(k, 2), pl.ds(q * 2, 2)], e_out.at[:, :, cols(q, k)], recv.at[OUTL, k])

    def a_local():
        return pltpu.make_async_copy(blocks, a_buf.at[pl.ds(q * slots, slots)], a_recv.at[0])

    def a_remote():
        mine = a_buf.at[pl.ds(q * slots, slots)]
        return pltpu.make_async_remote_copy(
            src_ref=blocks, dst_ref=mine, send_sem=a_send.at[0], recv_sem=a_recv.at[1],
            device_id=dev_core, device_id_type=MESH)

    def start(copies):
        for copy in copies:
            copy.start()

    barrier = pltpu.get_barrier_semaphore()
    others = plane + line
    for dev in others:
        pl.semaphore_signal(barrier, inc=1, device_id=dev, device_id_type=MESH)
    pl.semaphore_wait(barrier, len(others))

    def stage_a(k):
        own_copy(k).wait()
        arrived(CORE, k, piece(k, i, (1 - q) * 2, 2), dev_core)
        x_copy(k).start()
        start(y_copies(k))

    def stage_b(k):
        arrived(X, k, piece(k, xi), dev_x)
        start(yx_copies(k))

    def stage_c(k):
        arrived(YPA, k, piece(k, ym), dev_ym)
        arrived(YMA, k, piece(k, yp), dev_yp)
        start(fwd_copies(k))
        arrived(YPB, k, piece(k, xym), dev_ym)
        arrived(YMB, k, piece(k, xyp), dev_yp)
        start(fwdx_copies(k))

    def partial(r):
        return q_buf[tab[4 * slots + r]]

    def compute(k):
        arrived(YPC, k, piece(k, y2, 0, 2), dev_ym)
        arrived(YMC, k, piece(k, y2, 2, 2), dev_yp)
        arrived(YPD, k, piece(k, xy2, 0, 2), dev_ym)
        arrived(YMD, k, piece(k, xy2, 2, 2), dev_yp)
        move = pltpu.make_async_copy(b_buf.at[k], b_cmp, cmp_sem.at[0])
        move.start()
        move.wait()

        def product(p, _):
            q_buf[p + 1] = keep[p] * q_buf[p] + jnp.dot(
                a_buf[tab[p]], b_cmp[tab[2 * slots + p]], preferred_element_type=jnp.float32)
            return 0

        lax.fori_loop(0, 2 * slots, product, 0, unroll=8)

        slot = lax.rem(k, 2)

        @pl.when(k >= 2)
        def _():
            x1_copy(k - 2).wait_send()
            for copy in m1_copies(k - 2) + m2a_copies(k - 2):
                copy.wait_send()

        def pack0(n, _):
            x1s[slot, n] = encode(partial((1 - xh) * 16 + n * 4 + 3))
            return 0

        lax.fori_loop(0, 4, pack0, 0)
        x1_copy(k).start()

        def pack1(n, _):
            m1s[slot, 0, n] = encode(partial(z2 * 4 + n))
            m1s[slot, 1, n] = encode(partial(16 + z2 * 4 + n))
            return 0

        lax.fori_loop(0, 3, pack1, 0)
        start(m1_copies(k))

        def pack2(n, _):
            m2as[slot, 0, n] = encode(partial(16 + zp * 4 + n))
            m2as[slot, 1, n] = encode(partial(zm * 4 + n))
            return 0

        lax.fori_loop(0, 3, pack2, 0)
        start(m2a_copies(k))

        keep_slot = lax.rem(k, 3)

        def hold(n, _):
            t_buf[0, n] = partial(zp * 4 + n)
            t_buf[1, n] = partial(16 + zm * 4 + n)
            s_buf[keep_slot, 0, n] = partial(z * 4 + n)
            s_buf[keep_slot, 1, n] = partial(16 + z * 4 + n)
            return 0

        lax.fori_loop(0, 3, hold, 0)

        def hold_last(n, _):
            u_buf[n] = partial(xh * 16 + n * 4 + 3)
            return 0

        lax.fori_loop(0, 4, hold_last, 0)

    def relay(k):
        slot = lax.rem(k, 2)
        keep_slot = lax.rem(k, 3)

        @pl.when(k >= 2)
        def _():
            for copy in m2b_copies(k - 2) + ea_copies(k - 2):
                copy.wait_send()

        arrived(M1P, k, m1r.at[k, 0], dev_zm)
        arrived(M1M, k, m1r.at[k, 1], dev_zp)

        def pack(n, _):
            for d in range(2):
                m2bs[slot, d, n] = encode(t_buf[d, n] + decode(m1r[k, d, n]))
            return 0

        lax.fori_loop(0, 3, pack, 0)
        start(m2b_copies(k))

        arrived(X1, k, x1r.at[k], dev_x2)

        def join(n, _):
            v_buf[keep_slot, n] = u_buf[n] + decode(x1r[k, n])
            return 0

        lax.fori_loop(0, 4, join, 0)
        eas[slot, 0, 0] = encode(v_buf[keep_slot, z2, LOW])
        eas[slot, 0, 1] = encode(v_buf[keep_slot, zp, HIGH])
        eas[slot, 1, 0] = encode(v_buf[keep_slot, z2, HIGH])
        eas[slot, 1, 1] = encode(v_buf[keep_slot, zm, LOW])
        start(ea_copies(k))

    def collect(k):
        slot = lax.rem(k, 2)
        keep_slot = lax.rem(k, 3)

        @pl.when(k >= 2)
        def _():
            mx_copy(k - 2).wait_send()
            for copy in eb_copies(k - 2):
                copy.wait_send()

        arrived(M2AP, k, m2ar.at[k, 0], dev_zm)
        arrived(M2AM, k, m2ar.at[k, 1], dev_zp)
        arrived(M2BP, k, m2br.at[k, 0], dev_zm)
        arrived(M2BM, k, m2br.at[k, 1], dev_zp)

        def total(h, n):
            return s_buf[keep_slot, h, n] + (decode(m2br[k, h, n]) + decode(m2ar[k, 1 - h, n]))

        def pack(n, _):
            mxs[slot, n] = encode(total(1 - xh, n))
            return 0

        lax.fori_loop(0, 3, pack, 0)
        mx_copy(k).start()

        arrived(EAP, k, ear.at[k, 0], dev_zm)
        arrived(EAM, k, ear.at[k, 1], dev_zp)
        ebs[slot, 0] = encode(v_buf[keep_slot, zp, LOW] + decode(ear[k, 0, 0]))
        ebs[slot, 1] = encode(v_buf[keep_slot, zm, HIGH] + decode(ear[k, 1, 0]))
        start(eb_copies(k))

        def hold(n, _):
            s_buf[keep_slot, xh, n] = total(xh, n)
            return 0

        lax.fori_loop(0, 3, hold, 0)

    lane_row = lax.broadcasted_iota(jnp.int32, (8, LANES), 0)

    def finish(k):
        slot = lax.rem(k, 2)
        keep_slot = lax.rem(k, 3)

        @pl.when(k >= 2)
        def _():
            outc_copy(k - 2).wait_send()
            outl_copy(k - 2).wait()

        arrived(EBP, k, ebr.at[k, 0], dev_zm)
        arrived(EBM, k, ebr.at[k, 1], dev_zp)
        low = v_buf[keep_slot, z, LOW] + (decode(ebr[k, 0]) + decode(ear[k, 1, 1]))
        high = v_buf[keep_slot, z, HIGH] + (decode(ebr[k, 1]) + decode(ear[k, 0, 1]))
        fin[slot, 3, LOW] = low
        fin[slot, 3, HIGH] = high
        acc = jnp.sum((low * low + high * high).reshape(-1, 8, LANES), axis=0)

        arrived(MX, k, mxr.at[k], dev_x2)

        def add(n, acc):
            value = s_buf[keep_slot, xh, n] + decode(mxr[k, n])
            fin[slot, n] = value
            return acc + jnp.sum((value * value).reshape(-1, 8, LANES), axis=0)

        acc = lax.fori_loop(0, 3, add, acc)
        outc_copy(k).start()
        outl_copy(k).start()
        ms[0] = jnp.where(lane_row == k, jnp.sum(acc, axis=0, keepdims=True), ms[0])

    def first(k, _):
        own_copy(k).start()
        core_copy(k).start()
        return 0

    lax.fori_loop(0, 2, first, 0)
    a_local().start()
    a_remote().start()
    lax.fori_loop(2, chunks, first, 0)
    q_buf[0] = jnp.zeros(q_buf.shape[1:], jnp.float32)
    ms[0] = jnp.zeros((8, LANES), jnp.float32)

    stage_a(0)
    stage_b(0)
    stage_a(1)
    a_local().wait()
    pltpu.make_async_remote_copy(
        src_ref=blocks, dst_ref=a_buf.at[pl.ds((1 - q) * slots, slots)], send_sem=a_send.at[0],
        recv_sem=a_recv.at[1], device_id=dev_core, device_id_type=MESH).wait_recv()

    def step(t, _):
        @pl.when(t < chunks)
        def _():
            stage_c(t)

        @pl.when(t + 1 < chunks)
        def _():
            stage_b(t + 1)

        @pl.when(t + 2 < chunks)
        def _():
            stage_a(t + 2)

        @pl.when((t >= 1) & (t - 1 < chunks))
        def _():
            relay(t - 1)

        @pl.when((t >= 2) & (t - 2 < chunks))
        def _():
            collect(t - 2)

        @pl.when(t >= 3)
        def _():
            finish(t - 3)

        @pl.when(t < chunks)
        def _():
            compute(t)

        return 0

    lax.fori_loop(0, chunks + 3, step, 0)

    copies = [pltpu.make_async_remote_copy(
        src_ref=ms.at[0], dst_ref=mr_plane.at[n], send_sem=mass_send.at[n], recv_sem=mass_recv.at[n],
        device_id=dev, device_id_type=MESH) for n, dev in enumerate(plane)]
    start(copies)
    for copy in copies:
        copy.wait()
    ms[1] = ms[0] + jnp.sum(mr_plane[...], axis=0)
    copies = [pltpu.make_async_remote_copy(
        src_ref=ms.at[1], dst_ref=mr_line.at[n], send_sem=mass_send.at[15 + n], recv_sem=mass_recv.at[15 + n],
        device_id=dev, device_id_type=MESH) for n, dev in enumerate(line)]
    start(copies)
    for copy in copies:
        copy.wait()
    mass_out[q] = ms[1] + jnp.sum(mr_line[0:3], axis=0)
    mass_out[1 - q] = jnp.sum(mr_line[3:7], axis=0)

    a_remote().wait_send()

    def drain(k, _):
        core_copy(k).wait_send()
        x_copy(k).wait_send()
        for copy in y_copies(k) + yx_copies(k) + fwd_copies(k) + fwdx_copies(k):
            copy.wait_send()
        arrived(OUTC, k, e_out.at[:, :, cols(1 - q, k)], dev_core)
        return 0

    lax.fori_loop(0, chunks, drain, 0)

    def drain_last(k, _):
        for copy in m1_copies(k) + m2a_copies(k) + m2b_copies(k) + ea_copies(k) + eb_copies(k):
            copy.wait_send()
        x1_copy(k).wait_send()
        mx_copy(k).wait_send()
        outc_copy(k).wait_send()
        outl_copy(k).wait()
        return 0

    lax.fori_loop(chunks - 2, chunks, drain_last, 0)


def tables(block_rows, block_cols, live_count):
    slots = block_rows.shape[-1]
    q = lax.axis_index("col") % 2
    rows = block_rows.reshape(slots) - lax.axis_index("row") * 32
    cols = block_cols.reshape(slots)
    c = cols // 2 // 16 * 2 + cols % 2
    place = c // 2 * 4 + q * 2 + c % 2
    key = jnp.where(jnp.arange(slots) < live_count.reshape(()), rows, 32)
    mine = jnp.stack([key, place])
    other = lax.ppermute(mine, "col", [(n, n + 1 - 2 * (n % 2)) for n in range(16)])
    key = jnp.concatenate([mine[0], other[0]])
    place = jnp.concatenate([mine[1], other[1]])
    number = jnp.arange(2 * slots)
    block = jnp.where(number < slots, q * slots + number, (1 - q) * slots + number - slots)
    before = (key[:, None] < key[None, :]) | ((key[:, None] == key[None, :]) & (number[:, None] < number[None, :]))
    rank = jnp.sum(before, axis=0)
    hit = rank[None, :] == number[:, None]
    block = jnp.sum(jnp.where(hit, block[None, :], 0), axis=1)
    place = jnp.sum(jnp.where(hit, place[None, :], 0), axis=1)
    again = jnp.any((rank[None, :] + 1 == rank[:, None]) & (key[None, :] == key[:, None]), axis=1)
    keep = jnp.any(hit & again[None, :], axis=1).astype(jnp.float32)
    row = jnp.arange(32)
    upto = jnp.sum(key[None, :] <= row[:, None], axis=1)
    last = jnp.where(jnp.any(key[None, :] == row[:, None], axis=1), upto, 0)
    return jnp.concatenate([block, place, last]).astype(jnp.int32), keep


def body(blocks, block_rows, block_cols, live_count, slab):
    slots, bs = blocks.shape[2], blocks.shape[3]
    depth, width = slab.shape
    chunks = width // 2 // LANES
    tab, keep = tables(block_rows, block_cols, live_count)
    f32, bf16 = jnp.float32, jnp.bfloat16
    tile, half = (bs, LANES), (bs // 2, LANES)
    vm = pltpu.VMEM
    e, mass = pl.pallas_call(
        functools.partial(kernel, chunks, slots),
        out_shape=(jax.ShapeDtypeStruct((2, bs, width), f32), jax.ShapeDtypeStruct((2, chunks, LANES), f32)),
        in_specs=[pl.BlockSpec(memory_space=pltpu.SMEM), pl.BlockSpec(memory_space=pltpu.SMEM),
                  pl.BlockSpec(memory_space=pl.ANY), pl.BlockSpec(memory_space=pl.ANY)],
        out_specs=(pl.BlockSpec(memory_space=pl.ANY), pl.BlockSpec(memory_space=pltpu.VMEM)),
        scratch_shapes=[
            vm((2 * slots, bs, bs), bf16),
            vm((chunks, 32) + tile, bf16),
            vm((32,) + tile, bf16),
            vm((2 * slots + 1,) + tile, f32),
            vm((3, 2, 3) + tile, f32),
            vm((2, 3) + tile, f32),
            vm((2, 2, 3) + tile, bf16), vm((chunks, 2, 3) + tile, bf16),
            vm((2, 2, 3) + tile, bf16), vm((chunks, 2, 3) + tile, bf16),
            vm((2, 2, 3) + tile, bf16), vm((chunks, 2, 3) + tile, bf16),
            vm((2, 3) + tile, bf16), vm((chunks, 3) + tile, bf16),
            vm((2, 4) + tile, bf16), vm((chunks, 4) + tile, bf16),
            vm((2, 2, 2) + half, bf16), vm((chunks, 2, 2) + half, bf16),
            vm((2, 2) + half, bf16), vm((chunks, 2) + half, bf16),
            vm((4,) + tile, f32), vm((3, 4) + tile, f32),
            vm((2, 4) + tile, f32),
            vm((2, chunks, LANES), f32), vm((15, chunks, LANES), f32), vm((7, chunks, LANES), f32),
            pltpu.SemaphoreType.DMA((KINDS, chunks)), pltpu.SemaphoreType.DMA((KINDS, chunks)),
            pltpu.SemaphoreType.DMA((1,)), pltpu.SemaphoreType.DMA((2,)),
            pltpu.SemaphoreType.DMA((22,)), pltpu.SemaphoreType.DMA((22,)),
            pltpu.SemaphoreType.DMA((1,)),
        ],
        compiler_params=pltpu.CompilerParams(
            collective_id=0, has_side_effects=True, vmem_limit_bytes=58 * 1024 * 1024),
        cost_estimate=pl.CostEstimate(
            flops=2 * 2 * slots * bs * bs * width // 2, bytes_accessed=16 * 2**20, transcendentals=0),
    )(tab, keep, blocks.reshape(slots, bs, bs), slab.reshape(2, bs, width))
    scale = depth * 128 / mass.reshape(1, 1, width)
    return (e * e * scale).reshape(depth, width)


def solution(mesh):
    placed = (
        P("row", "col", None, None, None),
        P("row", "col", None),
        P("row", "col", None),
        P("row", "col"),
        P(("row", "col"), None),
    )
    return jax.shard_map(
        body, mesh=mesh, in_specs=placed, out_specs=P(("row", "col"), None), check_vma=False
    )
```

```python
import functools

import jax
import jax.numpy as jnp
from jax import lax
from jax.experimental import pallas as pl
from jax.experimental.pallas import tpu as pltpu
from jax.sharding import PartitionSpec as P

MESH = pl.DeviceIdType.MESH
LOW, HIGH = pl.ds(0, 128), pl.ds(128, 128)

LANES = 128
FORKED = 4
MID, POWER, FLOOR = 6.0, 26.0, 117.0
LN2 = 0.6931471805599453

(OWN, CORE, OUTC, OUTL,
 X, YPA, YMA, YPB, YMB, YPC, YMC, YPD, YMD, XF0, XF1,
 M1P, M1M, M2AP, M2AM, M2BP, M2BM, MX, X1, EAP, EAM, EBP, EBM) = range(27)
WIDE, KINDS, TURNS = 4, 27, 4


def encode(x):
    u = jnp.log(x) * (1.0 / LN2) - MID
    y = jnp.exp2(jnp.abs(u) * POWER - FLOOR)
    return jnp.where(x > 0.0, jnp.where(u < 0.0, -y, y), 0.0).astype(jnp.bfloat16)


def decode(y):
    y = y.astype(jnp.float32)
    u = jnp.log(jnp.abs(y)) * (1.0 / (POWER * LN2)) + FLOOR / POWER
    return jnp.where(y != 0.0, jnp.exp2(jnp.where(y < 0.0, -u, u) + MID), 0.0)


def kernel(chunks, slots, tab, keep, blocks, slab, e_out, mass_out,
           a_buf, b_buf, b_cmp, q_buf, s_buf, t_buf,
           m1s, m1r, m2as, m2ar, m2bs, m2br, mxs, mxr, x1s, x1r, eas, ear, ebs, ebr, u_buf, v_buf,
           fin, ms, mr_plane, mr_line,
           wide_send, wide_recv, send, recv, a_send, a_recv, mass_send, mass_recv, cmp_sem):
    i = lax.axis_index("row")
    j = lax.axis_index("col")
    y = lax.rem(i, 4)
    yb = i - y
    q = lax.rem(j, 2)
    z = lax.rem(j // 2, 4)
    xh = j // 8
    zb = xh * 8 + q

    def row_y(d):
        return yb + lax.rem(y + d, 4)

    def col_z(d):
        return zb + 2 * lax.rem(z + d, 4)

    def flip(r):
        return lax.rem(r + 4, 8)

    xi = flip(i)
    yp, y2, ym = row_y(1), row_y(2), row_y(3)
    xyp, xy2, xym = flip(yp), flip(y2), flip(ym)
    jc = j + 1 - 2 * q
    jx = lax.rem(j + 8, 16)
    zp, z2, zm = lax.rem(z + 1, 4), lax.rem(z + 2, 4), lax.rem(z + 3, 4)

    dev_core = (i, jc)
    dev_x = (xi, j)
    dev_x2 = (i, jx)
    dev_yp, dev_ym = (yp, j), (ym, j)
    dev_zp, dev_zm = (i, col_z(1)), (i, col_z(3))
    plane = [(lax.rem(yb + 4 * fx, 8) + lax.rem(y + d, 4), lax.rem(j + 8 * fh, 16))
             for fx in range(2) for d in range(4) for fh in range(2)][1:]
    line = [(i, col_z(d)) for d in (1, 2, 3)] + [(i, col_z(d) + 1 - 2 * q) for d in range(4)]

    def cols(half, k):
        return pl.ds(pl.multiple_of(half * (chunks * LANES) + k * LANES, LANES), LANES)

    def remote(kind, k, src, dst, dev):
        if kind < WIDE:
            sems = wide_send.at[kind, k], wide_recv.at[kind, k]
        else:
            sems = send.at[kind - WIDE, lax.rem(k, TURNS)], recv.at[kind - WIDE, lax.rem(k, TURNS)]
        return pltpu.make_async_remote_copy(
            src_ref=src, dst_ref=dst, send_sem=sems[0], recv_sem=sems[1], device_id=dev, device_id_type=MESH)

    def arrived(kind, k, ref, dev):
        remote(kind, k, ref, ref, dev).wait_recv()

    def piece(k, r, first=0, count=4):
        return b_buf.at[k, pl.ds(r * 4 + first, count)]

    def own_copy(k):
        return pltpu.make_async_copy(slab.at[:, :, cols(q, k)], piece(k, i, q * 2, 2), wide_recv.at[OWN, k])

    def core_copy(k):
        return remote(CORE, k, slab.at[:, :, cols(1 - q, k)], piece(k, i, q * 2, 2), dev_core)

    def piece_copy(kind, k, r, dev, first=0, count=4):
        return remote(kind, k, piece(k, r, first, count), piece(k, r, first, count), dev)

    def x_copy(k):
        return piece_copy(X, k, i, dev_x)

    def y_copies(k):
        return [piece_copy(YPA, k, i, dev_yp), piece_copy(YMA, k, i, dev_ym)]

    def yx_copies(k, forked):
        if forked:
            return [piece_copy(YPB, k, xi, dev_yp, 0, 3), piece_copy(YMB, k, xi, dev_ym, 1, 3)]
        return [piece_copy(YPB, k, xi, dev_yp), piece_copy(YMB, k, xi, dev_ym)]

    def fork_copies(k):
        return [piece_copy(XF0, k, ym, dev_x, 3, 1), piece_copy(XF1, k, yp, dev_x, 0, 1)]

    def by_fork(k, act):
        @pl.when(k < FORKED)
        def _():
            act(True)

        @pl.when(k >= FORKED)
        def _():
            act(False)

    def fwd_copies(k):
        return [piece_copy(YPC, k, ym, dev_yp, 0, 2), piece_copy(YMC, k, yp, dev_ym, 2, 2)]

    def fwdx_copies(k):
        return [piece_copy(YPD, k, xym, dev_yp, 0, 2), piece_copy(YMD, k, xyp, dev_ym, 2, 2)]

    def pair_copies(kp, k, src, dst):
        slot = lax.rem(k, 2)
        return [remote(kp, k, src.at[slot, 0], dst.at[k, 0], dev_zp),
                remote(kp + 1, k, src.at[slot, 1], dst.at[k, 1], dev_zm)]

    def m1_copies(k):
        return pair_copies(M1P, k, m1s, m1r)

    def m2a_copies(k):
        return pair_copies(M2AP, k, m2as, m2ar)

    def m2b_copies(k):
        return pair_copies(M2BP, k, m2bs, m2br)

    def x1_copy(k):
        return remote(X1, k, x1s.at[lax.rem(k, 2)], x1r.at[k], dev_x2)

    def ea_copies(k):
        return pair_copies(EAP, k, eas, ear)

    def eb_copies(k):
        return pair_copies(EBP, k, ebs, ebr)

    def mx_copy(k):
        return remote(MX, k, mxs.at[lax.rem(k, 2)], mxr.at[k], dev_x2)

    def outc_copy(k):
        return remote(OUTC, k, fin.at[lax.rem(k, 2), pl.ds((1 - q) * 2, 2)], e_out.at[:, :, cols(q, k)], dev_core)

    def outl_copy(k):
        return pltpu.make_async_copy(fin.at[lax.rem(k, 2), pl.ds(q * 2, 2)], e_out.at[:, :, cols(q, k)], wide_recv.at[OUTL, k])

    def a_local():
        return pltpu.make_async_copy(blocks, a_buf.at[pl.ds(q * slots, slots)], a_recv.at[0])

    def a_remote():
        mine = a_buf.at[pl.ds(q * slots, slots)]
        return pltpu.make_async_remote_copy(
            src_ref=blocks, dst_ref=mine, send_sem=a_send.at[0], recv_sem=a_recv.at[1],
            device_id=dev_core, device_id_type=MESH)

    def start(copies):
        for copy in copies:
            copy.start()

    def sent(copies):
        for copy in copies:
            copy.wait_send()

    def first(k, _):
        core_copy(k).start()
        return 0

    def first_local(k, _):
        own_copy(k).start()
        return 0

    lax.fori_loop(0, chunks, first_local, 0)
    barrier = pltpu.get_barrier_semaphore()
    others = plane + line
    for dev in others:
        pl.semaphore_signal(barrier, inc=1, device_id=dev, device_id_type=MESH)
    a_local().start()
    q_buf[0] = jnp.zeros(q_buf.shape[1:], jnp.float32)
    ms[0] = jnp.zeros((8, LANES), jnp.float32)
    pl.semaphore_wait(barrier, len(others))

    def stage_a(k):
        @pl.when(k >= TURNS)
        def _():
            sent([x_copy(k - TURNS)] + y_copies(k - TURNS))

        own_copy(k).wait()
        arrived(CORE, k, piece(k, i, (1 - q) * 2, 2), dev_core)
        start(y_copies(k))
        x_copy(k).start()

    def stage_b(k):
        @pl.when(k >= TURNS)
        def _():
            by_fork(k - TURNS, lambda forked: sent(yx_copies(k - TURNS, forked)))

        arrived(X, k, piece(k, xi), dev_x)
        by_fork(k, lambda forked: start(yx_copies(k, forked)))

    def stage_c(k):
        @pl.when(k >= TURNS)
        def _():
            sent(fwd_copies(k - TURNS) + fwdx_copies(k - TURNS))

            @pl.when(k - TURNS < FORKED)
            def _():
                sent(fork_copies(k - TURNS))

        arrived(YPA, k, piece(k, ym), dev_ym)
        arrived(YMA, k, piece(k, yp), dev_yp)
        start(fwd_copies(k))

        @pl.when(k < FORKED)
        def _():
            start(fork_copies(k))

        def rest(forked):
            arrived(YPB, k, piece(k, xym, 0, 3 if forked else 4), dev_ym)
            arrived(YMB, k, piece(k, xyp, *((1, 3) if forked else (0, 4))), dev_yp)

        by_fork(k, rest)
        start(fwdx_copies(k))

    def partial(r):
        return q_buf[tab[4 * slots + r]]

    def compute(k):
        arrived(YPC, k, piece(k, y2, 0, 2), dev_ym)
        arrived(YMC, k, piece(k, y2, 2, 2), dev_yp)
        arrived(YPD, k, piece(k, xy2, 0, 2), dev_ym)
        arrived(YMD, k, piece(k, xy2, 2, 2), dev_yp)

        @pl.when(k < FORKED)
        def _():
            arrived(XF0, k, piece(k, xym, 3, 1), dev_x)
            arrived(XF1, k, piece(k, xyp, 0, 1), dev_x)

        move = pltpu.make_async_copy(b_buf.at[k], b_cmp, cmp_sem.at[0])
        move.start()

        @pl.when(k == 0)
        def _():
            a_local().wait()
            pltpu.make_async_remote_copy(
                src_ref=blocks, dst_ref=a_buf.at[pl.ds((1 - q) * slots, slots)], send_sem=a_send.at[0],
                recv_sem=a_recv.at[1], device_id=dev_core, device_id_type=MESH).wait_recv()

        move.wait()

        def product(p, _):
            q_buf[p + 1] = keep[p] * q_buf[p] + jnp.dot(
                a_buf[tab[p]], b_cmp[tab[2 * slots + p]], preferred_element_type=jnp.float32)
            return 0

        lax.fori_loop(0, 2 * slots, product, 0, unroll=8)

        slot = lax.rem(k, 2)

        @pl.when(k >= 2)
        def _():
            x1_copy(k - 2).wait_send()
            for copy in m1_copies(k - 2) + m2a_copies(k - 2):
                copy.wait_send()

        def pack0(n, _):
            x1s[slot, n] = encode(partial((1 - xh) * 16 + n * 4 + 3))
            return 0

        lax.fori_loop(0, 4, pack0, 0)
        x1_copy(k).start()

        def pack1(n, _):
            m1s[slot, 0, n] = encode(partial(z2 * 4 + n))
            m1s[slot, 1, n] = encode(partial(16 + z2 * 4 + n))
            return 0

        lax.fori_loop(0, 3, pack1, 0)
        start(m1_copies(k))

        def pack2(n, _):
            m2as[slot, 0, n] = encode(partial(16 + zp * 4 + n))
            m2as[slot, 1, n] = encode(partial(zm * 4 + n))
            return 0

        lax.fori_loop(0, 3, pack2, 0)
        start(m2a_copies(k))

        keep_slot = lax.rem(k, 3)

        def hold(n, _):
            t_buf[0, n] = partial(zp * 4 + n)
            t_buf[1, n] = partial(16 + zm * 4 + n)
            s_buf[keep_slot, 0, n] = partial(z * 4 + n)
            s_buf[keep_slot, 1, n] = partial(16 + z * 4 + n)
            return 0

        lax.fori_loop(0, 3, hold, 0)

        def hold_last(n, _):
            u_buf[n] = partial(xh * 16 + n * 4 + 3)
            return 0

        lax.fori_loop(0, 4, hold_last, 0)

    def relay(k):
        slot = lax.rem(k, 2)
        keep_slot = lax.rem(k, 3)

        @pl.when(k >= 2)
        def _():
            for copy in m2b_copies(k - 2) + ea_copies(k - 2):
                copy.wait_send()

        arrived(M1P, k, m1r.at[k, 0], dev_zm)
        arrived(M1M, k, m1r.at[k, 1], dev_zp)

        def pack(n, _):
            for d in range(2):
                m2bs[slot, d, n] = encode(t_buf[d, n] + decode(m1r[k, d, n]))
            return 0

        lax.fori_loop(0, 3, pack, 0)
        start(m2b_copies(k))

        arrived(X1, k, x1r.at[k], dev_x2)

        def join(n, _):
            v_buf[keep_slot, n] = u_buf[n] + decode(x1r[k, n])
            return 0

        lax.fori_loop(0, 4, join, 0)
        eas[slot, 0, 0] = encode(v_buf[keep_slot, z2, LOW])
        eas[slot, 0, 1] = encode(v_buf[keep_slot, zp, HIGH])
        eas[slot, 1, 0] = encode(v_buf[keep_slot, z2, HIGH])
        eas[slot, 1, 1] = encode(v_buf[keep_slot, zm, LOW])
        start(ea_copies(k))

    def collect(k):
        slot = lax.rem(k, 2)
        keep_slot = lax.rem(k, 3)

        @pl.when(k >= 2)
        def _():
            mx_copy(k - 2).wait_send()
            for copy in eb_copies(k - 2):
                copy.wait_send()

        arrived(M2AP, k, m2ar.at[k, 0], dev_zm)
        arrived(M2AM, k, m2ar.at[k, 1], dev_zp)
        arrived(M2BP, k, m2br.at[k, 0], dev_zm)
        arrived(M2BM, k, m2br.at[k, 1], dev_zp)

        def total(h, n):
            return s_buf[keep_slot, h, n] + (decode(m2br[k, h, n]) + decode(m2ar[k, 1 - h, n]))

        def pack(n, _):
            mxs[slot, n] = encode(total(1 - xh, n))
            return 0

        lax.fori_loop(0, 3, pack, 0)
        mx_copy(k).start()

        arrived(EAP, k, ear.at[k, 0], dev_zm)
        arrived(EAM, k, ear.at[k, 1], dev_zp)
        ebs[slot, 0] = encode(v_buf[keep_slot, zp, LOW] + decode(ear[k, 0, 0]))
        ebs[slot, 1] = encode(v_buf[keep_slot, zm, HIGH] + decode(ear[k, 1, 0]))
        start(eb_copies(k))

        def hold(n, _):
            s_buf[keep_slot, xh, n] = total(xh, n)
            return 0

        lax.fori_loop(0, 3, hold, 0)

    lane_row = lax.broadcasted_iota(jnp.int32, (8, LANES), 0)

    def finish(k):
        slot = lax.rem(k, 2)
        keep_slot = lax.rem(k, 3)

        @pl.when(k >= 2)
        def _():
            outc_copy(k - 2).wait_send()
            outl_copy(k - 2).wait()

        arrived(EBP, k, ebr.at[k, 0], dev_zm)
        arrived(EBM, k, ebr.at[k, 1], dev_zp)
        low = v_buf[keep_slot, z, LOW] + (decode(ebr[k, 0]) + decode(ear[k, 1, 1]))
        high = v_buf[keep_slot, z, HIGH] + (decode(ebr[k, 1]) + decode(ear[k, 0, 1]))
        fin[slot, 3, LOW] = low
        fin[slot, 3, HIGH] = high
        acc = jnp.sum((low * low + high * high).reshape(-1, 8, LANES), axis=0)

        arrived(MX, k, mxr.at[k], dev_x2)

        def add(n, acc):
            value = s_buf[keep_slot, xh, n] + decode(mxr[k, n])
            fin[slot, n] = value
            return acc + jnp.sum((value * value).reshape(-1, 8, LANES), axis=0)

        acc = lax.fori_loop(0, 3, add, acc)
        outc_copy(k).start()
        outl_copy(k).start()
        ms[0] = jnp.where(lane_row == k, jnp.sum(acc, axis=0, keepdims=True), ms[0])

    core_copy(0).start()
    core_copy(1).start()
    a_remote().start()
    lax.fori_loop(2, chunks, first, 0)
    stage_a(0)
    stage_b(0)
    stage_a(1)

    def step(t, _):
        @pl.when(t < chunks)
        def _():
            stage_c(t)

        @pl.when(t + 1 < chunks)
        def _():
            stage_b(t + 1)

        @pl.when(t + 2 < chunks)
        def _():
            stage_a(t + 2)

        @pl.when((t >= 1) & (t - 1 < chunks))
        def _():
            relay(t - 1)

        @pl.when((t >= 2) & (t - 2 < chunks))
        def _():
            collect(t - 2)

        @pl.when(t >= 3)
        def _():
            finish(t - 3)

        @pl.when(t < chunks)
        def _():
            compute(t)

        return 0

    lax.fori_loop(0, chunks + 3, step, 0)

    copies = [pltpu.make_async_remote_copy(
        src_ref=ms.at[0], dst_ref=mr_plane.at[n], send_sem=mass_send.at[n], recv_sem=mass_recv.at[n],
        device_id=dev, device_id_type=MESH) for n, dev in enumerate(plane)]
    start(copies)
    for copy in copies:
        copy.wait()
    ms[1] = ms[0] + jnp.sum(mr_plane[...], axis=0)
    copies = [pltpu.make_async_remote_copy(
        src_ref=ms.at[1], dst_ref=mr_line.at[n], send_sem=mass_send.at[15 + n], recv_sem=mass_recv.at[15 + n],
        device_id=dev, device_id_type=MESH) for n, dev in enumerate(line)]
    start(copies)
    for copy in copies:
        copy.wait()
    mass_out[q] = ms[1] + jnp.sum(mr_line[0:3], axis=0)
    mass_out[1 - q] = jnp.sum(mr_line[3:7], axis=0)

    a_remote().wait_send()

    def drain(k, _):
        core_copy(k).wait_send()
        arrived(OUTC, k, e_out.at[:, :, cols(1 - q, k)], dev_core)
        return 0

    lax.fori_loop(0, chunks, drain, 0)

    def drain_pieces(k, _):
        sent([x_copy(k)] + y_copies(k) + fwd_copies(k) + fwdx_copies(k))
        by_fork(k, lambda forked: sent(yx_copies(k, forked) + (fork_copies(k) if forked else [])))
        return 0

    lax.fori_loop(chunks - TURNS, chunks, drain_pieces, 0)

    def drain_last(k, _):
        for copy in m1_copies(k) + m2a_copies(k) + m2b_copies(k) + ea_copies(k) + eb_copies(k):
            copy.wait_send()
        x1_copy(k).wait_send()
        mx_copy(k).wait_send()
        outc_copy(k).wait_send()
        outl_copy(k).wait()
        return 0

    lax.fori_loop(chunks - 2, chunks, drain_last, 0)


def tables(block_rows, block_cols, live_count):
    slots = block_rows.shape[-1]
    q = lax.axis_index("col") % 2
    rows = block_rows.reshape(slots) - lax.axis_index("row") * 32
    cols = block_cols.reshape(slots)
    c = cols // 2 // 16 * 2 + cols % 2
    place = c // 2 * 4 + q * 2 + c % 2
    key = jnp.where(jnp.arange(slots) < live_count.reshape(()), rows, 32)
    mine = jnp.stack([key, place])
    other = lax.ppermute(mine, "col", [(n, n + 1 - 2 * (n % 2)) for n in range(16)])
    key = jnp.concatenate([mine[0], other[0]])
    place = jnp.concatenate([mine[1], other[1]])
    number = jnp.arange(2 * slots)
    block = jnp.where(number < slots, q * slots + number, (1 - q) * slots + number - slots)
    before = (key[:, None] < key[None, :]) | ((key[:, None] == key[None, :]) & (number[:, None] < number[None, :]))
    rank = jnp.sum(before, axis=0)
    hit = rank[None, :] == number[:, None]
    block = jnp.sum(jnp.where(hit, block[None, :], 0), axis=1)
    place = jnp.sum(jnp.where(hit, place[None, :], 0), axis=1)
    again = jnp.any((rank[None, :] + 1 == rank[:, None]) & (key[None, :] == key[:, None]), axis=1)
    keep = jnp.any(hit & again[None, :], axis=1).astype(jnp.float32)
    row = jnp.arange(32)
    upto = jnp.sum(key[None, :] <= row[:, None], axis=1)
    last = jnp.where(jnp.any(key[None, :] == row[:, None], axis=1), upto, 0)
    return jnp.concatenate([block, place, last]).astype(jnp.int32), keep


def body(blocks, block_rows, block_cols, live_count, slab):
    slots, bs = blocks.shape[2], blocks.shape[3]
    depth, width = slab.shape
    chunks = width // 2 // LANES
    tab, keep = tables(block_rows, block_cols, live_count)
    f32, bf16 = jnp.float32, jnp.bfloat16
    tile, half = (bs, LANES), (bs // 2, LANES)
    vm = pltpu.VMEM
    e, mass = pl.pallas_call(
        functools.partial(kernel, chunks, slots),
        out_shape=(jax.ShapeDtypeStruct((2, bs, width), f32), jax.ShapeDtypeStruct((2, chunks, LANES), f32)),
        in_specs=[pl.BlockSpec(memory_space=pltpu.SMEM), pl.BlockSpec(memory_space=pltpu.SMEM),
                  pl.BlockSpec(memory_space=pl.ANY), pl.BlockSpec(memory_space=pl.ANY)],
        out_specs=(pl.BlockSpec(memory_space=pl.ANY), pl.BlockSpec(memory_space=pltpu.VMEM)),
        scratch_shapes=[
            vm((2 * slots, bs, bs), bf16),
            vm((chunks, 32) + tile, bf16),
            vm((32,) + tile, bf16),
            vm((2 * slots + 1,) + tile, f32),
            vm((3, 2, 3) + tile, f32),
            vm((2, 3) + tile, f32),
            vm((2, 2, 3) + tile, bf16), vm((chunks, 2, 3) + tile, bf16),
            vm((2, 2, 3) + tile, bf16), vm((chunks, 2, 3) + tile, bf16),
            vm((2, 2, 3) + tile, bf16), vm((chunks, 2, 3) + tile, bf16),
            vm((2, 3) + tile, bf16), vm((chunks, 3) + tile, bf16),
            vm((2, 4) + tile, bf16), vm((chunks, 4) + tile, bf16),
            vm((2, 2, 2) + half, bf16), vm((chunks, 2, 2) + half, bf16),
            vm((2, 2) + half, bf16), vm((chunks, 2) + half, bf16),
            vm((4,) + tile, f32), vm((3, 4) + tile, f32),
            vm((2, 4) + tile, f32),
            vm((2, chunks, LANES), f32), vm((15, chunks, LANES), f32), vm((7, chunks, LANES), f32),
            pltpu.SemaphoreType.DMA((WIDE, chunks)), pltpu.SemaphoreType.DMA((WIDE, chunks)),
            pltpu.SemaphoreType.DMA((KINDS - WIDE, TURNS)), pltpu.SemaphoreType.DMA((KINDS - WIDE, TURNS)),
            pltpu.SemaphoreType.DMA((1,)), pltpu.SemaphoreType.DMA((2,)),
            pltpu.SemaphoreType.DMA((22,)), pltpu.SemaphoreType.DMA((22,)),
            pltpu.SemaphoreType.DMA((1,)),
        ],
        compiler_params=pltpu.CompilerParams(
            collective_id=0, has_side_effects=True, vmem_limit_bytes=58 * 1024 * 1024),
        cost_estimate=pl.CostEstimate(
            flops=2 * 2 * slots * bs * bs * width // 2, bytes_accessed=16 * 2**20, transcendentals=0),
    )(tab, keep, blocks.reshape(slots, bs, bs), slab.reshape(2, bs, width))
    scale = depth * 128 / mass.reshape(1, 1, width)
    return (e * e * scale).reshape(depth, width)


def solution(mesh):
    placed = (
        P("row", "col", None, None, None),
        P("row", "col", None),
        P("row", "col", None),
        P("row", "col"),
        P(("row", "col"), None),
    )
    return jax.shard_map(
        body, mesh=mesh, in_specs=placed, out_specs=P(("row", "col"), None), check_vma=False
    )
```

```python
import functools

import jax
import jax.numpy as jnp
from jax import lax
from jax.experimental import pallas as pl
from jax.experimental.pallas import tpu as pltpu
from jax.sharding import PartitionSpec as P

MESH = pl.DeviceIdType.MESH
LOW, HIGH = pl.ds(0, 128), pl.ds(128, 128)

LANES = 128
FORKED = 4
MID, POWER, FLOOR = 6.0, 26.0, 117.0
LN2 = 0.6931471805599453

(OWN, CORE, OUTC, OUTL,
 X, YPA, YMA, YPB, YMB, YPC, YMC, YPD, YMD, XF0, XF1,
 M1P, M1M, M2AP, M2AM, M2BP, M2BM, MX, X1, EAP, EAM, EBP, EBM) = range(27)
WIDE, KINDS, TURNS = 4, 27, 4


def encode(x):
    u = jnp.log(x) * (1.0 / LN2) - MID
    y = jnp.exp2(jnp.abs(u) * POWER - FLOOR)
    return jnp.where(x > 0.0, jnp.where(u < 0.0, -y, y), 0.0).astype(jnp.bfloat16)


def decode(y):
    y = y.astype(jnp.float32)
    u = jnp.log(jnp.abs(y)) * (1.0 / (POWER * LN2)) + FLOOR / POWER
    return jnp.where(y != 0.0, jnp.exp2(jnp.where(y < 0.0, -u, u) + MID), 0.0)


def kernel(chunks, slots, rows, columns, live, blocks, slab, e_out, mass_out,
           a_buf, b_buf, b_cmp, q_buf, s_buf, t_buf,
           m1s, m1r, m2as, m2ar, m2bs, m2br, mxs, mxr, x1s, x1r, eas, ear, ebs, ebr, u_buf, v_buf,
           fin, ms, mr_plane, mr_line,
           meta, meta_in, tab_v, keep_v, tab, keep,
           wide_send, wide_recv, send, recv, a_send, a_recv, mass_send, mass_recv, cmp_sem, meta_sems, tab_sems):
    i = lax.axis_index("row")
    j = lax.axis_index("col")
    y = lax.rem(i, 4)
    yb = i - y
    q = lax.rem(j, 2)
    z = lax.rem(j // 2, 4)
    xh = j // 8
    zb = xh * 8 + q

    def row_y(d):
        return yb + lax.rem(y + d, 4)

    def col_z(d):
        return zb + 2 * lax.rem(z + d, 4)

    def flip(r):
        return lax.rem(r + 4, 8)

    xi = flip(i)
    yp, y2, ym = row_y(1), row_y(2), row_y(3)
    xyp, xy2, xym = flip(yp), flip(y2), flip(ym)
    jc = j + 1 - 2 * q
    jx = lax.rem(j + 8, 16)
    zp, z2, zm = lax.rem(z + 1, 4), lax.rem(z + 2, 4), lax.rem(z + 3, 4)

    dev_core = (i, jc)
    dev_x = (xi, j)
    dev_x2 = (i, jx)
    dev_yp, dev_ym = (yp, j), (ym, j)
    dev_zp, dev_zm = (i, col_z(1)), (i, col_z(3))
    plane = [(lax.rem(yb + 4 * fx, 8) + lax.rem(y + d, 4), lax.rem(j + 8 * fh, 16))
             for fx in range(2) for d in range(4) for fh in range(2)][1:]
    line = [(i, col_z(d)) for d in (1, 2, 3)] + [(i, col_z(d) + 1 - 2 * q) for d in range(4)]

    def cols(half, k):
        return pl.ds(pl.multiple_of(half * (chunks * LANES) + k * LANES, LANES), LANES)

    def remote(kind, k, src, dst, dev):
        if kind < WIDE:
            sems = wide_send.at[kind, k], wide_recv.at[kind, k]
        else:
            sems = send.at[kind - WIDE, lax.rem(k, TURNS)], recv.at[kind - WIDE, lax.rem(k, TURNS)]
        return pltpu.make_async_remote_copy(
            src_ref=src, dst_ref=dst, send_sem=sems[0], recv_sem=sems[1], device_id=dev, device_id_type=MESH)

    def arrived(kind, k, ref, dev):
        remote(kind, k, ref, ref, dev).wait_recv()

    def piece(k, r, first=0, count=4):
        return b_buf.at[k, pl.ds(r * 4 + first, count)]

    def own_copy(k):
        return pltpu.make_async_copy(slab.at[:, :, cols(q, k)], piece(k, i, q * 2, 2), wide_recv.at[OWN, k])

    def core_copy(k):
        return remote(CORE, k, slab.at[:, :, cols(1 - q, k)], piece(k, i, q * 2, 2), dev_core)

    def piece_copy(kind, k, r, dev, first=0, count=4):
        return remote(kind, k, piece(k, r, first, count), piece(k, r, first, count), dev)

    def x_copy(k):
        return piece_copy(X, k, i, dev_x)

    def y_copies(k):
        return [piece_copy(YPA, k, i, dev_yp), piece_copy(YMA, k, i, dev_ym)]

    def yx_copies(k, forked):
        if forked:
            return [piece_copy(YPB, k, xi, dev_yp, 0, 3), piece_copy(YMB, k, xi, dev_ym, 1, 3)]
        return [piece_copy(YPB, k, xi, dev_yp), piece_copy(YMB, k, xi, dev_ym)]

    def fork_copies(k):
        return [piece_copy(XF0, k, ym, dev_x, 3, 1), piece_copy(XF1, k, yp, dev_x, 0, 1)]

    def by_fork(k, act):
        @pl.when(k < FORKED)
        def _():
            act(True)

        @pl.when(k >= FORKED)
        def _():
            act(False)

    def fwd_copies(k):
        return [piece_copy(YPC, k, ym, dev_yp, 0, 2), piece_copy(YMC, k, yp, dev_ym, 2, 2)]

    def fwdx_copies(k):
        return [piece_copy(YPD, k, xym, dev_yp, 0, 2), piece_copy(YMD, k, xyp, dev_ym, 2, 2)]

    def pair_copies(kp, k, src, dst):
        slot = lax.rem(k, 2)
        return [remote(kp, k, src.at[slot, 0], dst.at[k, 0], dev_zp),
                remote(kp + 1, k, src.at[slot, 1], dst.at[k, 1], dev_zm)]

    def m1_copies(k):
        return pair_copies(M1P, k, m1s, m1r)

    def m2a_copies(k):
        return pair_copies(M2AP, k, m2as, m2ar)

    def m2b_copies(k):
        return pair_copies(M2BP, k, m2bs, m2br)

    def x1_copy(k):
        return remote(X1, k, x1s.at[lax.rem(k, 2)], x1r.at[k], dev_x2)

    def ea_copies(k):
        return pair_copies(EAP, k, eas, ear)

    def eb_copies(k):
        return pair_copies(EBP, k, ebs, ebr)

    def mx_copy(k):
        return remote(MX, k, mxs.at[lax.rem(k, 2)], mxr.at[k], dev_x2)

    def outc_copy(k):
        return remote(OUTC, k, fin.at[lax.rem(k, 2), pl.ds((1 - q) * 2, 2)], e_out.at[:, :, cols(q, k)], dev_core)

    def outl_copy(k):
        return pltpu.make_async_copy(fin.at[lax.rem(k, 2), pl.ds(q * 2, 2)], e_out.at[:, :, cols(q, k)], wide_recv.at[OUTL, k])

    def a_local():
        return pltpu.make_async_copy(blocks, a_buf.at[pl.ds(q * slots, slots)], a_recv.at[0])

    def a_remote():
        mine = a_buf.at[pl.ds(q * slots, slots)]
        return pltpu.make_async_remote_copy(
            src_ref=blocks, dst_ref=mine, send_sem=a_send.at[0], recv_sem=a_recv.at[1],
            device_id=dev_core, device_id_type=MESH)

    def start(copies):
        for copy in copies:
            copy.start()

    def sent(copies):
        for copy in copies:
            copy.wait_send()

    def first(k, _):
        core_copy(k).start()
        return 0

    def first_local(k, _):
        own_copy(k).start()
        return 0

    def meta_copy():
        return pltpu.make_async_remote_copy(
            src_ref=meta, dst_ref=meta_in, send_sem=meta_sems.at[0], recv_sem=meta_sems.at[1],
            device_id=dev_core, device_id_type=MESH)

    lane = lax.broadcasted_iota(jnp.int32, (8, LANES), 1)

    def list_slots():
        number = lax.broadcasted_iota(jnp.int32, (1, slots), 1)
        key = jnp.where(number < live[0, 0], rows[...] - i * 32, 32)
        place = lax.shift_right_logical(columns[...], 5) * 4 + q * 2 + (columns[...] & 1)
        meta[...] = jnp.full((8, LANES), 64, jnp.int32)

        @pl.when(q == 0)
        def _():
            meta[0:1, 0:slots] = key
            meta[1:2, 0:slots] = place

        @pl.when(q == 1)
        def _():
            meta[0:1, slots:2 * slots] = key
            meta[1:2, slots:2 * slots] = place

    def make_tables():
        meta_copy().wait()
        joint = jnp.where((lane >= q * slots) & (lane < (q + 1) * slots), meta[...], meta_in[...])
        square = (LANES, LANES)
        item = lax.broadcasted_iota(jnp.int32, square, 0)
        at = lax.broadcasted_iota(jnp.int32, square, 1)
        key_b = jnp.broadcast_to(joint[0:1], square)
        key_a = key_b.T
        place_a = jnp.broadcast_to(joint[1:2], square).T

        def count(mask):
            return jnp.sum(jnp.where(mask, 1, 0), axis=0, keepdims=True)

        def pick(mask, value):
            return jnp.sum(jnp.where(mask, value, 0), axis=0, keepdims=True)

        rank = count((key_a < key_b) | ((key_a == key_b) & (item < at)))
        rank_a = jnp.broadcast_to(rank, square).T
        hit = rank_a == at
        key_here = pick(hit, key_a)
        key_before = pick(rank_a + 1 == at, key_a)
        tab_v[...] = jnp.zeros((8, LANES), jnp.int32)
        tab_v[0:1] = pick(hit, item)
        tab_v[1:2] = pick(hit, place_a)
        tab_v[2:3] = jnp.where(count(key_a == at) > 0, count(key_a <= at), 0)
        keep_v[...] = jnp.broadcast_to(
            jnp.where((key_here == key_before) & (lane[0:1] > 0), 1.0, 0.0), (8, LANES))
        moves = [pltpu.make_async_copy(tab_v, tab, tab_sems.at[0]), pltpu.make_async_copy(keep_v, keep, tab_sems.at[1])]
        start(moves)
        for move in moves:
            move.wait()

    lax.fori_loop(0, chunks, first_local, 0)
    barrier = pltpu.get_barrier_semaphore()
    others = plane + line
    for dev in others:
        pl.semaphore_signal(barrier, inc=1, device_id=dev, device_id_type=MESH)
    a_local().start()
    q_buf[0] = jnp.zeros(q_buf.shape[1:], jnp.float32)
    ms[0] = jnp.zeros((8, LANES), jnp.float32)
    list_slots()
    pl.semaphore_wait(barrier, len(others))
    meta_copy().start()

    def stage_a(k):
        @pl.when(k >= TURNS)
        def _():
            sent([x_copy(k - TURNS)] + y_copies(k - TURNS))

        own_copy(k).wait()
        arrived(CORE, k, piece(k, i, (1 - q) * 2, 2), dev_core)
        start(y_copies(k))
        x_copy(k).start()

    def stage_b(k):
        @pl.when(k >= TURNS)
        def _():
            by_fork(k - TURNS, lambda forked: sent(yx_copies(k - TURNS, forked)))

        arrived(X, k, piece(k, xi), dev_x)
        by_fork(k, lambda forked: start(yx_copies(k, forked)))

    def stage_c(k):
        @pl.when(k >= TURNS)
        def _():
            sent(fwd_copies(k - TURNS) + fwdx_copies(k - TURNS))

            @pl.when(k - TURNS < FORKED)
            def _():
                sent(fork_copies(k - TURNS))

        arrived(YPA, k, piece(k, ym), dev_ym)
        arrived(YMA, k, piece(k, yp), dev_yp)
        start(fwd_copies(k))

        @pl.when(k < FORKED)
        def _():
            start(fork_copies(k))

        def rest(forked):
            arrived(YPB, k, piece(k, xym, 0, 3 if forked else 4), dev_ym)
            arrived(YMB, k, piece(k, xyp, *((1, 3) if forked else (0, 4))), dev_yp)

        by_fork(k, rest)
        start(fwdx_copies(k))

    def partial(r):
        return q_buf[tab[2, r]]

    def compute(k):
        arrived(YPC, k, piece(k, y2, 0, 2), dev_ym)
        arrived(YMC, k, piece(k, y2, 2, 2), dev_yp)
        arrived(YPD, k, piece(k, xy2, 0, 2), dev_ym)
        arrived(YMD, k, piece(k, xy2, 2, 2), dev_yp)

        @pl.when(k < FORKED)
        def _():
            arrived(XF0, k, piece(k, xym, 3, 1), dev_x)
            arrived(XF1, k, piece(k, xyp, 0, 1), dev_x)

        move = pltpu.make_async_copy(b_buf.at[k], b_cmp, cmp_sem.at[0])
        move.start()

        @pl.when(k == 0)
        def _():
            a_local().wait()
            pltpu.make_async_remote_copy(
                src_ref=blocks, dst_ref=a_buf.at[pl.ds((1 - q) * slots, slots)], send_sem=a_send.at[0],
                recv_sem=a_recv.at[1], device_id=dev_core, device_id_type=MESH).wait_recv()

        move.wait()

        def product(p, _):
            q_buf[p + 1] = keep[0, p] * q_buf[p] + jnp.dot(
                a_buf[tab[0, p]], b_cmp[tab[1, p]], preferred_element_type=jnp.float32)
            return 0

        lax.fori_loop(0, 2 * slots, product, 0, unroll=8)

        slot = lax.rem(k, 2)

        @pl.when(k >= 2)
        def _():
            x1_copy(k - 2).wait_send()
            for copy in m1_copies(k - 2) + m2a_copies(k - 2):
                copy.wait_send()

        def pack0(n, _):
            x1s[slot, n] = encode(partial((1 - xh) * 16 + n * 4 + 3))
            return 0

        lax.fori_loop(0, 4, pack0, 0)
        x1_copy(k).start()

        def pack1(n, _):
            m1s[slot, 0, n] = encode(partial(z2 * 4 + n))
            m1s[slot, 1, n] = encode(partial(16 + z2 * 4 + n))
            return 0

        lax.fori_loop(0, 3, pack1, 0)
        start(m1_copies(k))

        def pack2(n, _):
            m2as[slot, 0, n] = encode(partial(16 + zp * 4 + n))
            m2as[slot, 1, n] = encode(partial(zm * 4 + n))
            return 0

        lax.fori_loop(0, 3, pack2, 0)

        @pl.when(k == chunks - 1)
        def _():
            sent(m1_copies(k))

        start(m2a_copies(k))

        keep_slot = lax.rem(k, 3)

        def hold(n, _):
            t_buf[0, n] = partial(zp * 4 + n)
            t_buf[1, n] = partial(16 + zm * 4 + n)
            s_buf[keep_slot, 0, n] = partial(z * 4 + n)
            s_buf[keep_slot, 1, n] = partial(16 + z * 4 + n)
            return 0

        lax.fori_loop(0, 3, hold, 0)

        def hold_last(n, _):
            u_buf[n] = partial(xh * 16 + n * 4 + 3)
            return 0

        lax.fori_loop(0, 4, hold_last, 0)

    def relay(k):
        slot = lax.rem(k, 2)
        keep_slot = lax.rem(k, 3)

        @pl.when(k >= 2)
        def _():
            for copy in m2b_copies(k - 2) + ea_copies(k - 2):
                copy.wait_send()

        arrived(M1P, k, m1r.at[k, 0], dev_zm)
        arrived(M1M, k, m1r.at[k, 1], dev_zp)

        def pack(n, _):
            for d in range(2):
                m2bs[slot, d, n] = encode(t_buf[d, n] + decode(m1r[k, d, n]))
            return 0

        lax.fori_loop(0, 3, pack, 0)
        start(m2b_copies(k))

        arrived(X1, k, x1r.at[k], dev_x2)

        def join(n, _):
            v_buf[keep_slot, n] = u_buf[n] + decode(x1r[k, n])
            return 0

        lax.fori_loop(0, 4, join, 0)
        eas[slot, 0, 0] = encode(v_buf[keep_slot, z2, LOW])
        eas[slot, 0, 1] = encode(v_buf[keep_slot, zp, HIGH])
        eas[slot, 1, 0] = encode(v_buf[keep_slot, z2, HIGH])
        eas[slot, 1, 1] = encode(v_buf[keep_slot, zm, LOW])
        start(ea_copies(k))

    def collect(k):
        slot = lax.rem(k, 2)
        keep_slot = lax.rem(k, 3)

        @pl.when(k >= 2)
        def _():
            mx_copy(k - 2).wait_send()
            for copy in eb_copies(k - 2):
                copy.wait_send()

        arrived(M2AP, k, m2ar.at[k, 0], dev_zm)
        arrived(M2AM, k, m2ar.at[k, 1], dev_zp)
        arrived(M2BP, k, m2br.at[k, 0], dev_zm)
        arrived(M2BM, k, m2br.at[k, 1], dev_zp)

        def total(h, n):
            return s_buf[keep_slot, h, n] + (decode(m2br[k, h, n]) + decode(m2ar[k, 1 - h, n]))

        def pack(n, _):
            mxs[slot, n] = encode(total(1 - xh, n))
            return 0

        lax.fori_loop(0, 3, pack, 0)
        mx_copy(k).start()

        arrived(EAP, k, ear.at[k, 0], dev_zm)
        arrived(EAM, k, ear.at[k, 1], dev_zp)
        ebs[slot, 0] = encode(v_buf[keep_slot, zp, LOW] + decode(ear[k, 0, 0]))
        ebs[slot, 1] = encode(v_buf[keep_slot, zm, HIGH] + decode(ear[k, 1, 0]))
        start(eb_copies(k))

        def hold(n, _):
            s_buf[keep_slot, xh, n] = total(xh, n)
            return 0

        lax.fori_loop(0, 3, hold, 0)

    lane_row = lax.broadcasted_iota(jnp.int32, (8, LANES), 0)

    def finish(k):
        slot = lax.rem(k, 2)
        keep_slot = lax.rem(k, 3)

        @pl.when(k >= 2)
        def _():
            outc_copy(k - 2).wait_send()
            outl_copy(k - 2).wait()

        arrived(EBP, k, ebr.at[k, 0], dev_zm)
        arrived(EBM, k, ebr.at[k, 1], dev_zp)
        low = v_buf[keep_slot, z, LOW] + (decode(ebr[k, 0]) + decode(ear[k, 1, 1]))
        high = v_buf[keep_slot, z, HIGH] + (decode(ebr[k, 1]) + decode(ear[k, 0, 1]))
        fin[slot, 3, LOW] = low
        fin[slot, 3, HIGH] = high
        acc = jnp.sum((low * low + high * high).reshape(-1, 8, LANES), axis=0)

        arrived(MX, k, mxr.at[k], dev_x2)

        def add(n, acc):
            value = s_buf[keep_slot, xh, n] + decode(mxr[k, n])
            fin[slot, n] = value
            return acc + jnp.sum((value * value).reshape(-1, 8, LANES), axis=0)

        acc = lax.fori_loop(0, 3, add, acc)
        outc_copy(k).start()
        outl_copy(k).start()
        ms[0] = jnp.where(lane_row == k, jnp.sum(acc, axis=0, keepdims=True), ms[0])

    core_copy(0).start()
    core_copy(1).start()
    a_remote().start()
    lax.fori_loop(2, chunks, first, 0)
    stage_a(0)
    stage_b(0)
    stage_a(1)
    make_tables()

    def step(t, _):
        @pl.when(t < chunks)
        def _():
            stage_c(t)

        @pl.when(t + 1 < chunks)
        def _():
            stage_b(t + 1)

        @pl.when(t + 2 < chunks)
        def _():
            stage_a(t + 2)

        @pl.when((t >= 1) & (t - 1 < chunks))
        def _():
            relay(t - 1)

        @pl.when((t >= 2) & (t - 2 < chunks))
        def _():
            collect(t - 2)

        @pl.when(t >= 3)
        def _():
            finish(t - 3)

        @pl.when(t < chunks)
        def _():
            compute(t)

        return 0

    lax.fori_loop(0, chunks + 3, step, 0)

    copies = [pltpu.make_async_remote_copy(
        src_ref=ms.at[0], dst_ref=mr_plane.at[n], send_sem=mass_send.at[n], recv_sem=mass_recv.at[n],
        device_id=dev, device_id_type=MESH) for n, dev in enumerate(plane)]
    start(copies)
    for copy in copies:
        copy.wait()
    ms[1] = ms[0] + jnp.sum(mr_plane[...], axis=0)
    copies = [pltpu.make_async_remote_copy(
        src_ref=ms.at[1], dst_ref=mr_line.at[n], send_sem=mass_send.at[15 + n], recv_sem=mass_recv.at[15 + n],
        device_id=dev, device_id_type=MESH) for n, dev in enumerate(line)]
    start(copies)
    for copy in copies:
        copy.wait()
    mass_out[q] = ms[1] + jnp.sum(mr_line[0:3], axis=0)
    mass_out[1 - q] = jnp.sum(mr_line[3:7], axis=0)

    a_remote().wait_send()

    def drain(k, _):
        core_copy(k).wait_send()
        arrived(OUTC, k, e_out.at[:, :, cols(1 - q, k)], dev_core)
        return 0

    lax.fori_loop(0, chunks, drain, 0)

    def drain_pieces(k, _):
        sent([x_copy(k)] + y_copies(k) + fwd_copies(k) + fwdx_copies(k))
        by_fork(k, lambda forked: sent(yx_copies(k, forked) + (fork_copies(k) if forked else [])))
        return 0

    lax.fori_loop(chunks - TURNS, chunks, drain_pieces, 0)

    sent(m1_copies(chunks - 2))

    def drain_last(k, _):
        for copy in m2a_copies(k) + m2b_copies(k) + ea_copies(k) + eb_copies(k):
            copy.wait_send()
        x1_copy(k).wait_send()
        mx_copy(k).wait_send()
        outc_copy(k).wait_send()
        outl_copy(k).wait()
        return 0

    lax.fori_loop(chunks - 2, chunks, drain_last, 0)


def body(blocks, block_rows, block_cols, live_count, slab):
    slots, bs = blocks.shape[2], blocks.shape[3]
    depth, width = slab.shape
    chunks = width // 2 // LANES
    f32, bf16 = jnp.float32, jnp.bfloat16
    tile, half = (bs, LANES), (bs // 2, LANES)
    vm = pltpu.VMEM
    e, mass = pl.pallas_call(
        functools.partial(kernel, chunks, slots),
        out_shape=(jax.ShapeDtypeStruct((2, bs, width), f32), jax.ShapeDtypeStruct((2, chunks, LANES), f32)),
        in_specs=[pl.BlockSpec(memory_space=pltpu.VMEM), pl.BlockSpec(memory_space=pltpu.VMEM),
                  pl.BlockSpec(memory_space=pltpu.SMEM),
                  pl.BlockSpec(memory_space=pl.ANY), pl.BlockSpec(memory_space=pl.ANY)],
        out_specs=(pl.BlockSpec(memory_space=pl.ANY), pl.BlockSpec(memory_space=pltpu.VMEM)),
        scratch_shapes=[
            vm((2 * slots, bs, bs), bf16),
            vm((chunks, 32) + tile, bf16),
            vm((32,) + tile, bf16),
            vm((2 * slots + 1,) + tile, f32),
            vm((3, 2, 3) + tile, f32),
            vm((2, 3) + tile, f32),
            vm((2, 2, 3) + tile, bf16), vm((chunks, 2, 3) + tile, bf16),
            vm((2, 2, 3) + tile, bf16), vm((chunks, 2, 3) + tile, bf16),
            vm((2, 2, 3) + tile, bf16), vm((chunks, 2, 3) + tile, bf16),
            vm((2, 3) + tile, bf16), vm((chunks, 3) + tile, bf16),
            vm((2, 4) + tile, bf16), vm((chunks, 4) + tile, bf16),
            vm((2, 2, 2) + half, bf16), vm((chunks, 2, 2) + half, bf16),
            vm((2, 2) + half, bf16), vm((chunks, 2) + half, bf16),
            vm((4,) + tile, f32), vm((3, 4) + tile, f32),
            vm((2, 4) + tile, f32),
            vm((2, chunks, LANES), f32), vm((15, chunks, LANES), f32), vm((7, chunks, LANES), f32),
            vm((8, LANES), jnp.int32), vm((8, LANES), jnp.int32), vm((8, LANES), jnp.int32), vm((8, LANES), f32),
            pltpu.SMEM((8, LANES), jnp.int32), pltpu.SMEM((8, LANES), f32),
            pltpu.SemaphoreType.DMA((WIDE, chunks)), pltpu.SemaphoreType.DMA((WIDE, chunks)),
            pltpu.SemaphoreType.DMA((KINDS - WIDE, TURNS)), pltpu.SemaphoreType.DMA((KINDS - WIDE, TURNS)),
            pltpu.SemaphoreType.DMA((1,)), pltpu.SemaphoreType.DMA((2,)),
            pltpu.SemaphoreType.DMA((22,)), pltpu.SemaphoreType.DMA((22,)),
            pltpu.SemaphoreType.DMA((1,)), pltpu.SemaphoreType.DMA((2,)), pltpu.SemaphoreType.DMA((2,)),
        ],
        compiler_params=pltpu.CompilerParams(
            collective_id=0, has_side_effects=True, vmem_limit_bytes=58 * 1024 * 1024),
        cost_estimate=pl.CostEstimate(
            flops=2 * 2 * slots * bs * bs * width // 2, bytes_accessed=16 * 2**20, transcendentals=0),
    )(block_rows.reshape(1, slots), block_cols.reshape(1, slots), live_count, blocks.reshape(slots, bs, bs), slab.reshape(2, bs, width))
    scale = depth * 128 / mass.reshape(1, 1, width)
    return (e * e * scale).reshape(depth, width)


def solution(mesh):
    placed = (
        P("row", "col", None, None, None),
        P("row", "col", None),
        P("row", "col", None),
        P("row", "col"),
        P(("row", "col"), None),
    )
    return jax.shard_map(
        body, mesh=mesh, in_specs=placed, out_specs=P(("row", "col"), None), check_vma=False
    )
```

```python
import functools

import jax
import jax.numpy as jnp
from jax import lax
from jax.experimental import pallas as pl
from jax.experimental.pallas import tpu as pltpu
from jax.sharding import PartitionSpec as P

MESH = pl.DeviceIdType.MESH
LOW, HIGH = pl.ds(0, 128), pl.ds(128, 128)

LANES = 128
FORKED = 4
MID, POWER, FLOOR = 6.0, 26.0, 117.0
LN2 = 0.6931471805599453

(OWN, CORE, OUTC, OUTL,
 X, YPA, YMA, YPB, YMB, YPC, YMC, YPD, YMD, XF0, XF1,
 M1P, M1M, M2AP, M2AM, X1, EAP, EAM, EBP, EBM, M2BP, M2BM, MX) = range(27)
SPLIT = 3
WIDE, KINDS, TURNS = 4, 27 + 3 * (SPLIT - 1), 3


def encode(x):
    u = jnp.log(x) * (1.0 / LN2) - MID
    y = jnp.exp2(jnp.abs(u) * POWER - FLOOR)
    return jnp.where(x > 0.0, jnp.where(u < 0.0, -y, y), 0.0).astype(jnp.bfloat16)


def decode(y):
    y = y.astype(jnp.float32)
    u = jnp.log(jnp.abs(y)) * (1.0 / (POWER * LN2)) + FLOOR / POWER
    return jnp.exp2(jnp.where(y < 0.0, -u, u) + MID)


def kernel(chunks, slots, rows, columns, live, blocks, slab, e_out, mass_out,
           a_buf, b_buf, b_cmp, q_buf, s_buf, t_buf,
           m1s, m1r, m2as, m2ar, m2bs, m2br, mxs, mxr, x1s, x1r, eas, ear, ebs, ebr, u_buf, v_buf,
           fin, ms, mr_plane, mr_line,
           meta, meta_in, tab_v, keep_v, tab, keep,
           wide_send, wide_recv, send, recv, a_send, a_recv, mass_send, mass_recv, cmp_sem, meta_sems, tab_sems):
    i = lax.axis_index("row")
    j = lax.axis_index("col")
    y = lax.rem(i, 4)
    yb = i - y
    q = lax.rem(j, 2)
    z = lax.rem(j // 2, 4)
    xh = j // 8
    zb = xh * 8 + q

    def row_y(d):
        return yb + lax.rem(y + d, 4)

    def col_z(d):
        return zb + 2 * lax.rem(z + d, 4)

    def flip(r):
        return lax.rem(r + 4, 8)

    xi = flip(i)
    yp, y2, ym = row_y(1), row_y(2), row_y(3)
    xyp, xy2, xym = flip(yp), flip(y2), flip(ym)
    jc = j + 1 - 2 * q
    jx = lax.rem(j + 8, 16)
    zp, z2, zm = lax.rem(z + 1, 4), lax.rem(z + 2, 4), lax.rem(z + 3, 4)

    dev_core = (i, jc)
    dev_x = (xi, j)
    dev_x2 = (i, jx)
    dev_yp, dev_ym = (yp, j), (ym, j)
    dev_zp, dev_zm = (i, col_z(1)), (i, col_z(3))
    plane = [(lax.rem(yb + 4 * fx, 8) + lax.rem(y + d, 4), lax.rem(j + 8 * fh, 16))
             for fx in range(2) for d in range(4) for fh in range(2)][1:]
    line = [(i, col_z(d)) for d in (1, 2, 3)] + [(i, col_z(d) + 1 - 2 * q) for d in range(4)]

    def cols(half, k):
        return pl.ds(pl.multiple_of(half * (chunks * LANES) + k * LANES, LANES), LANES)

    def remote(kind, k, src, dst, dev):
        if kind < WIDE:
            sems = wide_send.at[kind - CORE, k], wide_recv.at[kind, k]
        else:
            sems = send.at[kind - WIDE, lax.rem(k, TURNS)], recv.at[kind - WIDE, lax.rem(k, TURNS)]
        return pltpu.make_async_remote_copy(
            src_ref=src, dst_ref=dst, send_sem=sems[0], recv_sem=sems[1], device_id=dev, device_id_type=MESH)

    def arrived(kind, k, ref, dev):
        remote(kind, k, ref, ref, dev).wait_recv()

    def piece(k, r, first=0, count=4):
        return b_buf.at[k, pl.ds(r * 4 + first, count)]

    def own_copy(k):
        return pltpu.make_async_copy(slab.at[:, :, cols(q, k)], piece(k, i, q * 2, 2), wide_recv.at[OWN, k])

    def core_copy(k):
        return remote(CORE, k, slab.at[:, :, cols(1 - q, k)], piece(k, i, q * 2, 2), dev_core)

    def piece_copy(kind, k, r, dev, first=0, count=4):
        return remote(kind, k, piece(k, r, first, count), piece(k, r, first, count), dev)

    def x_copy(k):
        return piece_copy(X, k, i, dev_x)

    def y_copies(k):
        return [piece_copy(YPA, k, i, dev_yp), piece_copy(YMA, k, i, dev_ym)]

    def yx_copies(k, forked):
        if forked:
            return [piece_copy(YPB, k, xi, dev_yp, 0, 3), piece_copy(YMB, k, xi, dev_ym, 1, 3)]
        return [piece_copy(YPB, k, xi, dev_yp), piece_copy(YMB, k, xi, dev_ym)]

    def fork_copies(k):
        return [piece_copy(XF0, k, ym, dev_x, 3, 1), piece_copy(XF1, k, yp, dev_x, 0, 1)]

    def by_fork(k, act):
        @pl.when(k < FORKED)
        def _():
            act(True)

        @pl.when(k >= FORKED)
        def _():
            act(False)

    def fwd_copies(k):
        return [piece_copy(YPC, k, ym, dev_yp, 0, 2), piece_copy(YMC, k, yp, dev_ym, 2, 2)]

    def fwdx_copies(k):
        return [piece_copy(YPD, k, xym, dev_yp, 0, 2), piece_copy(YMD, k, xyp, dev_ym, 2, 2)]

    def pair_copies(kp, k, src, dst):
        slot = lax.rem(k, 2)
        return [remote(kp, k, src.at[slot, 0], dst.at[k, 0], dev_zp),
                remote(kp + 1, k, src.at[slot, 1], dst.at[k, 1], dev_zm)]

    def m1_copies(k):
        return pair_copies(M1P, k, m1s, m1r)

    def m2a_copies(k):
        return pair_copies(M2AP, k, m2as, m2ar)

    def m2b_part(k, n):
        slot = lax.rem(k, 2)
        return [remote(M2BP + 3 * n, k, m2bs.at[slot, 0, n], m2br.at[k, 0, n], dev_zp),
                remote(M2BM + 3 * n, k, m2bs.at[slot, 1, n], m2br.at[k, 1, n], dev_zm)]

    def m2b_copies(k):
        return m2b_part(k, 0) + m2b_part(k, 1) + m2b_part(k, 2)

    def x1_copy(k):
        return remote(X1, k, x1s.at[lax.rem(k, 2)], x1r.at[k], dev_x2)

    def ea_copies(k):
        return pair_copies(EAP, k, eas, ear)

    def eb_copies(k):
        return pair_copies(EBP, k, ebs, ebr)

    def mx_part(k, n):
        return remote(MX + 3 * n, k, mxs.at[lax.rem(k, 2), n], mxr.at[k, n], dev_x2)

    def mx_copies(k):
        return [mx_part(k, n) for n in range(SPLIT)]

    def outc_copy(k):
        return remote(OUTC, k, fin.at[lax.rem(k, 2), pl.ds((1 - q) * 2, 2)], e_out.at[:, :, cols(q, k)], dev_core)

    def outl_copy(k):
        return pltpu.make_async_copy(fin.at[lax.rem(k, 2), pl.ds(q * 2, 2)], e_out.at[:, :, cols(q, k)], wide_recv.at[OUTL, k])

    def a_local():
        return pltpu.make_async_copy(blocks, a_buf.at[pl.ds(q * slots, slots)], a_recv.at[0])

    def a_remote():
        mine = a_buf.at[pl.ds(q * slots, slots)]
        return pltpu.make_async_remote_copy(
            src_ref=blocks, dst_ref=mine, send_sem=a_send.at[0], recv_sem=a_recv.at[1],
            device_id=dev_core, device_id_type=MESH)

    def start(copies):
        for copy in copies:
            copy.start()

    def sent(copies):
        for copy in copies:
            copy.wait_send()

    def first(k, _):
        core_copy(k).start()
        return 0

    def first_local(k, _):
        own_copy(k).start()
        return 0

    def meta_copy():
        return pltpu.make_async_remote_copy(
            src_ref=meta, dst_ref=meta_in, send_sem=meta_sems.at[0], recv_sem=meta_sems.at[1],
            device_id=dev_core, device_id_type=MESH)

    lane = lax.broadcasted_iota(jnp.int32, (8, LANES), 1)

    def list_slots():
        number = lax.broadcasted_iota(jnp.int32, (1, slots), 1)
        key = jnp.where(number < live[...], rows[...] - i * 32, 32)
        place = lax.shift_right_logical(columns[...], 5) * 4 + q * 2 + (columns[...] & 1)
        meta[...] = jnp.full((8, LANES), 64, jnp.int32)

        @pl.when(q == 0)
        def _():
            meta[0:1, 0:slots] = key
            meta[1:2, 0:slots] = place

        @pl.when(q == 1)
        def _():
            meta[0:1, slots:2 * slots] = key
            meta[1:2, slots:2 * slots] = place

    def make_tables():
        meta_copy().wait()
        joint = jnp.where((lane >= q * slots) & (lane < (q + 1) * slots), meta[...], meta_in[...])
        square = (LANES, LANES)
        item = lax.broadcasted_iota(jnp.int32, square, 0)
        at = lax.broadcasted_iota(jnp.int32, square, 1)
        key_b = jnp.broadcast_to(joint[0:1], square)
        key_a = key_b.T
        place_a = jnp.broadcast_to(joint[1:2], square).T

        def count(mask):
            return jnp.sum(jnp.where(mask, 1, 0), axis=0, keepdims=True)

        def pick(mask, value):
            return jnp.sum(jnp.where(mask, value, 0), axis=0, keepdims=True)

        rank = count((key_a < key_b) | ((key_a == key_b) & (item < at)))
        rank_a = jnp.broadcast_to(rank, square).T
        hit = rank_a == at
        key_here = pick(hit, key_a)
        key_before = pick(rank_a + 1 == at, key_a)
        tab_v[...] = jnp.zeros((8, LANES), jnp.int32)
        tab_v[0:1] = pick(hit, item)
        tab_v[1:2] = pick(hit, place_a)
        tab_v[2:3] = jnp.where(count(key_a == at) > 0, count(key_a <= at), 0)
        keep_v[...] = jnp.broadcast_to(
            jnp.where((key_here == key_before) & (lane[0:1] > 0), 1.0, 0.0), (8, LANES))
        moves = [pltpu.make_async_copy(tab_v, tab, tab_sems.at[0]), pltpu.make_async_copy(keep_v, keep, tab_sems.at[1])]
        start(moves)
        for move in moves:
            move.wait()

    lax.fori_loop(0, chunks, first_local, 0)
    barrier = pltpu.get_barrier_semaphore()
    others = plane + line
    for dev in others:
        pl.semaphore_signal(barrier, inc=1, device_id=dev, device_id_type=MESH)
    a_local().start()
    q_buf[0] = jnp.zeros(q_buf.shape[1:], jnp.float32)
    ms[0] = jnp.zeros((8, LANES), jnp.float32)
    list_slots()
    pl.semaphore_wait(barrier, len(others))
    meta_copy().start()

    def stage_a(k):
        @pl.when(k >= TURNS)
        def _():
            sent([x_copy(k - TURNS)] + y_copies(k - TURNS))

        own_copy(k).wait()
        arrived(CORE, k, piece(k, i, (1 - q) * 2, 2), dev_core)
        start(y_copies(k))
        x_copy(k).start()

    def stage_b(k):
        @pl.when(k >= TURNS)
        def _():
            by_fork(k - TURNS, lambda forked: sent(yx_copies(k - TURNS, forked)))

        arrived(X, k, piece(k, xi), dev_x)
        by_fork(k, lambda forked: start(yx_copies(k, forked)))

    def stage_c(k):
        @pl.when(k >= TURNS)
        def _():
            sent(fwd_copies(k - TURNS) + fwdx_copies(k - TURNS))

            @pl.when(k - TURNS < FORKED)
            def _():
                sent(fork_copies(k - TURNS))

        arrived(YPA, k, piece(k, ym), dev_ym)
        arrived(YMA, k, piece(k, yp), dev_yp)
        start(fwd_copies(k))

        @pl.when(k < FORKED)
        def _():
            start(fork_copies(k))

        def rest(forked):
            arrived(YPB, k, piece(k, xym, 0, 3 if forked else 4), dev_ym)
            arrived(YMB, k, piece(k, xyp, *((1, 3) if forked else (0, 4))), dev_yp)

        by_fork(k, rest)
        start(fwdx_copies(k))

    def partial(r):
        return q_buf[tab[2, r]]

    def compute(k):
        arrived(YPC, k, piece(k, y2, 0, 2), dev_ym)
        arrived(YMC, k, piece(k, y2, 2, 2), dev_yp)
        arrived(YPD, k, piece(k, xy2, 0, 2), dev_ym)
        arrived(YMD, k, piece(k, xy2, 2, 2), dev_yp)

        @pl.when(k < FORKED)
        def _():
            arrived(XF0, k, piece(k, xym, 3, 1), dev_x)
            arrived(XF1, k, piece(k, xyp, 0, 1), dev_x)

        move = pltpu.make_async_copy(b_buf.at[k], b_cmp, cmp_sem.at[0])
        move.start()

        @pl.when(k == 0)
        def _():
            a_local().wait()
            pltpu.make_async_remote_copy(
                src_ref=blocks, dst_ref=a_buf.at[pl.ds((1 - q) * slots, slots)], send_sem=a_send.at[0],
                recv_sem=a_recv.at[1], device_id=dev_core, device_id_type=MESH).wait_recv()

        move.wait()

        def product(p, _):
            q_buf[p + 1] = keep[0, p] * q_buf[p] + jnp.dot(
                a_buf[tab[0, p]], b_cmp[tab[1, p]], preferred_element_type=jnp.float32)
            return 0

        lax.fori_loop(0, 2 * slots, product, 0, unroll=8)

        slot = lax.rem(k, 2)

        @pl.when(k >= 2)
        def _():
            x1_copy(k - 2).wait_send()
            for copy in m1_copies(k - 2) + m2a_copies(k - 2):
                copy.wait_send()

        def pack0(n, _):
            x1s[slot, n] = encode(partial((1 - xh) * 16 + n * 4 + 3))
            return 0

        lax.fori_loop(0, 4, pack0, 0)
        x1_copy(k).start()

        def pack1(n, _):
            m1s[slot, 0, n] = encode(partial(z2 * 4 + n))
            m1s[slot, 1, n] = encode(partial(16 + z2 * 4 + n))
            return 0

        lax.fori_loop(0, 3, pack1, 0)
        start(m1_copies(k))

        def pack2(n, _):
            m2as[slot, 0, n] = encode(partial(16 + zp * 4 + n))
            m2as[slot, 1, n] = encode(partial(zm * 4 + n))
            return 0

        lax.fori_loop(0, 3, pack2, 0)

        @pl.when(k == chunks - 1)
        def _():
            sent(m1_copies(k))

        start(m2a_copies(k))

        keep_slot = lax.rem(k, 3)

        def hold(n, _):
            t_buf[0, n] = partial(zp * 4 + n)
            t_buf[1, n] = partial(16 + zm * 4 + n)
            s_buf[keep_slot, 0, n] = partial(z * 4 + n)
            s_buf[keep_slot, 1, n] = partial(16 + z * 4 + n)
            return 0

        lax.fori_loop(0, 3, hold, 0)

        def hold_last(n, _):
            u_buf[n] = partial(xh * 16 + n * 4 + 3)
            return 0

        lax.fori_loop(0, 4, hold_last, 0)

    def relay(k):
        slot = lax.rem(k, 2)
        keep_slot = lax.rem(k, 3)

        @pl.when(k >= 2)
        def _():
            for copy in m2b_copies(k - 2) + ea_copies(k - 2):
                copy.wait_send()

        arrived(M1P, k, m1r.at[k, 0], dev_zm)
        arrived(M1M, k, m1r.at[k, 1], dev_zp)

        for n in range(SPLIT):
            for d in range(2):
                m2bs[slot, d, n] = encode(t_buf[d, n] + decode(m1r[k, d, n]))
            start(m2b_part(k, n))

        arrived(X1, k, x1r.at[k], dev_x2)

        def join(n, _):
            v_buf[keep_slot, n] = u_buf[n] + decode(x1r[k, n])
            return 0

        lax.fori_loop(0, 4, join, 0)
        eas[slot, 0, 0] = encode(v_buf[keep_slot, z2, LOW])
        eas[slot, 0, 1] = encode(v_buf[keep_slot, zp, HIGH])
        eas[slot, 1, 0] = encode(v_buf[keep_slot, z2, HIGH])
        eas[slot, 1, 1] = encode(v_buf[keep_slot, zm, LOW])
        start(ea_copies(k))

    def collect(k):
        slot = lax.rem(k, 2)
        keep_slot = lax.rem(k, 3)

        @pl.when(k >= 2)
        def _():
            sent(mx_copies(k - 2) + eb_copies(k - 2))

        arrived(M2AP, k, m2ar.at[k, 0], dev_zm)
        arrived(M2AM, k, m2ar.at[k, 1], dev_zp)

        def total(h, n):
            return s_buf[keep_slot, h, n] + (decode(m2br[k, h, n]) + decode(m2ar[k, 1 - h, n]))

        for n in range(SPLIT):
            arrived(M2BP + 3 * n, k, m2br.at[k, 0, n], dev_zm)
            arrived(M2BM + 3 * n, k, m2br.at[k, 1, n], dev_zp)
            mxs[slot, n] = encode(total(1 - xh, n))
            mx_part(k, n).start()

        arrived(EAP, k, ear.at[k, 0], dev_zm)
        arrived(EAM, k, ear.at[k, 1], dev_zp)
        ebs[slot, 0] = encode(v_buf[keep_slot, zp, LOW] + decode(ear[k, 0, 0]))
        ebs[slot, 1] = encode(v_buf[keep_slot, zm, HIGH] + decode(ear[k, 1, 0]))
        start(eb_copies(k))

        def hold(n, _):
            s_buf[keep_slot, xh, n] = total(xh, n)
            return 0

        lax.fori_loop(0, 3, hold, 0)

    lane_row = lax.broadcasted_iota(jnp.int32, (8, LANES), 0)

    def finish(k):
        slot = lax.rem(k, 2)
        keep_slot = lax.rem(k, 3)

        @pl.when(k >= 2)
        def _():
            outc_copy(k - 2).wait_send()
            outl_copy(k - 2).wait()

        arrived(EBP, k, ebr.at[k, 0], dev_zm)
        arrived(EBM, k, ebr.at[k, 1], dev_zp)
        low = v_buf[keep_slot, z, LOW] + (decode(ebr[k, 0]) + decode(ear[k, 1, 1]))
        high = v_buf[keep_slot, z, HIGH] + (decode(ebr[k, 1]) + decode(ear[k, 0, 1]))
        fin[slot, 3, LOW] = low
        fin[slot, 3, HIGH] = high
        acc = jnp.sum((low * low + high * high).reshape(-1, 8, LANES), axis=0)

        for n in range(SPLIT):
            arrived(MX + 3 * n, k, mxr.at[k, n], dev_x2)
            value = s_buf[keep_slot, xh, n] + decode(mxr[k, n])
            fin[slot, n] = value
            acc = acc + jnp.sum((value * value).reshape(-1, 8, LANES), axis=0)

        outc_copy(k).start()
        outl_copy(k).start()
        ms[0] = jnp.where(lane_row == k, jnp.sum(acc, axis=0, keepdims=True), ms[0])

    core_copy(0).start()
    core_copy(1).start()
    a_remote().start()
    lax.fori_loop(2, chunks, first, 0)
    stage_a(0)
    stage_b(0)
    stage_a(1)
    make_tables()

    def step(t, _):
        @pl.when(t < chunks)
        def _():
            stage_c(t)

        @pl.when(t + 1 < chunks)
        def _():
            stage_b(t + 1)

        @pl.when(t + 2 < chunks)
        def _():
            stage_a(t + 2)

        @pl.when((t >= 1) & (t - 1 < chunks))
        def _():
            relay(t - 1)

        @pl.when((t >= 2) & (t - 2 < chunks))
        def _():
            collect(t - 2)

        @pl.when(t >= 3)
        def _():
            finish(t - 3)

        @pl.when(t < chunks)
        def _():
            compute(t)

        return 0

    lax.fori_loop(0, chunks + 3, step, 0)

    copies = [pltpu.make_async_remote_copy(
        src_ref=ms.at[0], dst_ref=mr_plane.at[n], send_sem=mass_send.at[n], recv_sem=mass_recv.at[n],
        device_id=dev, device_id_type=MESH) for n, dev in enumerate(plane)]
    start(copies)

    a_remote().wait_send()

    def drain(k, _):
        core_copy(k).wait_send()
        arrived(OUTC, k, e_out.at[:, :, cols(1 - q, k)], dev_core)
        return 0

    lax.fori_loop(0, chunks, drain, 0)

    def drain_pieces(k, _):
        sent([x_copy(k)] + y_copies(k) + fwd_copies(k) + fwdx_copies(k))
        by_fork(k, lambda forked: sent(yx_copies(k, forked) + (fork_copies(k) if forked else [])))
        return 0

    lax.fori_loop(chunks - TURNS, chunks, drain_pieces, 0)

    sent(m1_copies(chunks - 2))

    def drain_last(k, _):
        for copy in m2a_copies(k) + m2b_copies(k) + ea_copies(k) + eb_copies(k):
            copy.wait_send()
        x1_copy(k).wait_send()
        sent(mx_copies(k))
        outc_copy(k).wait_send()
        outl_copy(k).wait()
        return 0

    lax.fori_loop(chunks - 2, chunks, drain_last, 0)

    for copy in copies:
        copy.wait()
    ms[1] = ms[0] + jnp.sum(mr_plane[...], axis=0)
    copies = [pltpu.make_async_remote_copy(
        src_ref=ms.at[1], dst_ref=mr_line.at[n], send_sem=mass_send.at[15 + n], recv_sem=mass_recv.at[15 + n],
        device_id=dev, device_id_type=MESH) for n, dev in enumerate(line)]
    start(copies)
    for copy in copies:
        copy.wait()
    mass_out[q] = ms[1] + jnp.sum(mr_line[0:3], axis=0)
    mass_out[1 - q] = jnp.sum(mr_line[3:7], axis=0)


def body(blocks, block_rows, block_cols, live_count, slab):
    slots, bs = blocks.shape[2], blocks.shape[3]
    depth, width = slab.shape
    chunks = width // 2 // LANES
    f32, bf16 = jnp.float32, jnp.bfloat16
    tile, half = (bs, LANES), (bs // 2, LANES)
    vm = pltpu.VMEM
    e, mass = pl.pallas_call(
        functools.partial(kernel, chunks, slots),
        out_shape=(jax.ShapeDtypeStruct((2, bs, width), f32), jax.ShapeDtypeStruct((2, chunks, LANES), f32)),
        in_specs=[pl.BlockSpec(memory_space=pltpu.VMEM), pl.BlockSpec(memory_space=pltpu.VMEM),
                  pl.BlockSpec(memory_space=pltpu.VMEM),
                  pl.BlockSpec(memory_space=pl.ANY), pl.BlockSpec(memory_space=pl.ANY)],
        out_specs=(pl.BlockSpec(memory_space=pl.ANY), pl.BlockSpec(memory_space=pltpu.VMEM)),
        scratch_shapes=[
            vm((2 * slots, bs, bs), bf16),
            vm((chunks, 32) + tile, bf16),
            vm((32,) + tile, bf16),
            vm((2 * slots + 1,) + tile, f32),
            vm((3, 2, 3) + tile, f32),
            vm((2, 3) + tile, f32),
            vm((2, 2, 3) + tile, bf16), vm((chunks, 2, 3) + tile, bf16),
            vm((2, 2, 3) + tile, bf16), vm((chunks, 2, 3) + tile, bf16),
            vm((2, 2, 3) + tile, bf16), vm((chunks, 2, 3) + tile, bf16),
            vm((2, 3) + tile, bf16), vm((chunks, 3) + tile, bf16),
            vm((2, 4) + tile, bf16), vm((chunks, 4) + tile, bf16),
            vm((2, 2, 2) + half, bf16), vm((chunks, 2, 2) + half, bf16),
            vm((2, 2) + half, bf16), vm((chunks, 2) + half, bf16),
            vm((4,) + tile, f32), vm((3, 4) + tile, f32),
            vm((2, 4) + tile, f32),
            vm((2, chunks, LANES), f32), vm((15, chunks, LANES), f32), vm((7, chunks, LANES), f32),
            vm((8, LANES), jnp.int32), vm((8, LANES), jnp.int32), vm((8, LANES), jnp.int32), vm((8, LANES), f32),
            pltpu.SMEM((8, LANES), jnp.int32), pltpu.SMEM((8, LANES), f32),
            pltpu.SemaphoreType.DMA((2, chunks)), pltpu.SemaphoreType.DMA((WIDE, chunks)),
            pltpu.SemaphoreType.DMA((KINDS - WIDE, TURNS)), pltpu.SemaphoreType.DMA((KINDS - WIDE, TURNS)),
            pltpu.SemaphoreType.DMA((1,)), pltpu.SemaphoreType.DMA((2,)),
            pltpu.SemaphoreType.DMA((22,)), pltpu.SemaphoreType.DMA((22,)),
            pltpu.SemaphoreType.DMA((1,)), pltpu.SemaphoreType.DMA((2,)), pltpu.SemaphoreType.DMA((2,)),
        ],
        compiler_params=pltpu.CompilerParams(
            collective_id=0, has_side_effects=True, vmem_limit_bytes=58 * 1024 * 1024),
        cost_estimate=pl.CostEstimate(
            flops=2 * 2 * slots * bs * bs * width // 2, bytes_accessed=16 * 2**20, transcendentals=0),
    )(block_rows.reshape(1, slots), block_cols.reshape(1, slots), live_count, blocks.reshape(slots, bs, bs), slab.reshape(2, bs, width))
    scale = depth * 128 / mass.reshape(1, 1, width)
    return (e * e * scale).reshape(depth, width)


def solution(mesh):
    placed = (
        P("row", "col", None, None, None),
        P("row", "col", None),
        P("row", "col", None),
        P("row", "col"),
        P(("row", "col"), None),
    )
    return jax.shard_map(
        body, mesh=mesh, in_specs=placed, out_specs=P(("row", "col"), None), check_vma=False
    )
```

```python
import functools

import jax
import jax.numpy as jnp
from jax import lax
from jax.experimental import pallas as pl
from jax.experimental.pallas import tpu as pltpu
from jax.sharding import PartitionSpec as P

MESH = pl.DeviceIdType.MESH
LOW, HIGH = pl.ds(0, 128), pl.ds(128, 128)

LANES = 128
FORK_TWO, FORK_ONE = 2, 4
MID, POWER, FLOOR = 6.0, 26.0, 117.0
LN2 = 0.6931471805599453

(OWN, CORE, OUTC, OUTL,
 X, YPA, YMA, YPB, YMB, YPC, YMC, YPD, YMD, XF0, XF1,
 M1P, M1M, M2AP, M2AM, X1, EAP, EAM, EBP, EBM, M2BP, M2BM, MX) = range(27)
SPLIT = 3
WIDE, KINDS, TURNS = 4, 27 + 3 * (SPLIT - 1), 3


def encode(x):
    u = jnp.log(x) * (1.0 / LN2) - MID
    y = jnp.exp2(jnp.abs(u) * POWER - FLOOR)
    return jnp.where(x > 0.0, jnp.where(u < 0.0, -y, y), 0.0).astype(jnp.bfloat16)


def decode(y):
    y = y.astype(jnp.float32)
    u = jnp.log(jnp.abs(y)) * (1.0 / (POWER * LN2)) + FLOOR / POWER
    return jnp.exp2(jnp.where(y < 0.0, -u, u) + MID)


def kernel(chunks, slots, rows, columns, live, blocks, slab, e_out, mass_out,
           a_buf, b_buf, b_cmp, q_buf, s_buf, t_buf,
           m1s, m1r, m2as, m2ar, m2bs, m2br, mxs, mxr, x1s, x1r, eas, ear, ebs, ebr, u_buf, v_buf,
           fin, ms, mr_plane, mr_line,
           meta, meta_in, tab_v, keep_v, tab, keep,
           wide_send, wide_recv, send, recv, a_send, a_recv, mass_send, mass_recv, cmp_sem, meta_sems, tab_sems):
    i = lax.axis_index("row")
    j = lax.axis_index("col")
    y = lax.rem(i, 4)
    yb = i - y
    q = lax.rem(j, 2)
    z = lax.rem(j // 2, 4)
    xh = j // 8
    zb = xh * 8 + q

    def row_y(d):
        return yb + lax.rem(y + d, 4)

    def col_z(d):
        return zb + 2 * lax.rem(z + d, 4)

    def flip(r):
        return lax.rem(r + 4, 8)

    xi = flip(i)
    yp, y2, ym = row_y(1), row_y(2), row_y(3)
    xyp, xy2, xym = flip(yp), flip(y2), flip(ym)
    jc = j + 1 - 2 * q
    jx = lax.rem(j + 8, 16)
    zp, z2, zm = lax.rem(z + 1, 4), lax.rem(z + 2, 4), lax.rem(z + 3, 4)

    dev_core = (i, jc)
    dev_x = (xi, j)
    dev_x2 = (i, jx)
    dev_yp, dev_ym = (yp, j), (ym, j)
    dev_zp, dev_zm = (i, col_z(1)), (i, col_z(3))
    plane = [(lax.rem(yb + 4 * fx, 8) + lax.rem(y + d, 4), lax.rem(j + 8 * fh, 16))
             for fx in range(2) for d in range(4) for fh in range(2)][1:]
    line = [(i, col_z(d)) for d in (1, 2, 3)] + [(i, col_z(d) + 1 - 2 * q) for d in range(4)]

    def cols(half, k):
        return pl.ds(pl.multiple_of(half * (chunks * LANES) + k * LANES, LANES), LANES)

    def remote(kind, k, src, dst, dev):
        if kind < WIDE:
            sems = wide_send.at[kind - CORE, k], wide_recv.at[kind, k]
        else:
            sems = send.at[kind - WIDE, lax.rem(k, TURNS)], recv.at[kind - WIDE, lax.rem(k, TURNS)]
        return pltpu.make_async_remote_copy(
            src_ref=src, dst_ref=dst, send_sem=sems[0], recv_sem=sems[1], device_id=dev, device_id_type=MESH)

    def arrived(kind, k, ref, dev):
        remote(kind, k, ref, ref, dev).wait_recv()

    def piece(k, r, first=0, count=4):
        return b_buf.at[k, pl.ds(r * 4 + first, count)]

    def own_copy(k):
        return pltpu.make_async_copy(slab.at[:, :, cols(q, k)], piece(k, i, q * 2, 2), wide_recv.at[OWN, k])

    def core_copy(k):
        return remote(CORE, k, slab.at[:, :, cols(1 - q, k)], piece(k, i, q * 2, 2), dev_core)

    def piece_copy(kind, k, r, dev, first=0, count=4):
        return remote(kind, k, piece(k, r, first, count), piece(k, r, first, count), dev)

    def x_copy(k):
        return piece_copy(X, k, i, dev_x)

    def y_copies(k):
        return [piece_copy(YPA, k, i, dev_yp), piece_copy(YMA, k, i, dev_ym)]

    def yx_copies(k, forked):
        return [piece_copy(YPB, k, xi, dev_yp, 0, 4 - forked), piece_copy(YMB, k, xi, dev_ym, forked, 4 - forked)]

    def fork_copies(k, forked):
        if not forked:
            return []
        return [piece_copy(XF0, k, ym, dev_x, 4 - forked, forked), piece_copy(XF1, k, yp, dev_x, 0, forked)]

    def by_fork(k, act):
        @pl.when(k < FORK_TWO)
        def _():
            act(2)

        @pl.when((k >= FORK_TWO) & (k < FORK_ONE))
        def _():
            act(1)

        @pl.when(k >= FORK_ONE)
        def _():
            act(0)

    def fwd_copies(k):
        return [piece_copy(YPC, k, ym, dev_yp, 0, 2), piece_copy(YMC, k, yp, dev_ym, 2, 2)]

    def fwdx_copies(k):
        return [piece_copy(YPD, k, xym, dev_yp, 0, 2), piece_copy(YMD, k, xyp, dev_ym, 2, 2)]

    def pair_copies(kp, k, src, dst):
        slot = lax.rem(k, 2)
        return [remote(kp, k, src.at[slot, 0], dst.at[k, 0], dev_zp),
                remote(kp + 1, k, src.at[slot, 1], dst.at[k, 1], dev_zm)]

    def m1_copies(k):
        return pair_copies(M1P, k, m1s, m1r)

    def m2a_copies(k):
        return pair_copies(M2AP, k, m2as, m2ar)

    def m2b_part(k, n):
        slot = lax.rem(k, 2)
        return [remote(M2BP + 3 * n, k, m2bs.at[slot, 0, n], m2br.at[k, 0, n], dev_zp),
                remote(M2BM + 3 * n, k, m2bs.at[slot, 1, n], m2br.at[k, 1, n], dev_zm)]

    def m2b_copies(k):
        return m2b_part(k, 0) + m2b_part(k, 1) + m2b_part(k, 2)

    def x1_copy(k):
        return remote(X1, k, x1s.at[lax.rem(k, 2)], x1r.at[k], dev_x2)

    def ea_copies(k):
        return pair_copies(EAP, k, eas, ear)

    def eb_copies(k):
        return pair_copies(EBP, k, ebs, ebr)

    def mx_part(k, n):
        return remote(MX + 3 * n, k, mxs.at[lax.rem(k, 2), n], mxr.at[k, n], dev_x2)

    def mx_copies(k):
        return [mx_part(k, n) for n in range(SPLIT)]

    def outc_copy(k):
        return remote(OUTC, k, fin.at[lax.rem(k, 2), pl.ds((1 - q) * 2, 2)], e_out.at[:, :, cols(q, k)], dev_core)

    def outl_copy(k):
        return pltpu.make_async_copy(fin.at[lax.rem(k, 2), pl.ds(q * 2, 2)], e_out.at[:, :, cols(q, k)], wide_recv.at[OUTL, k])

    def a_local():
        return pltpu.make_async_copy(blocks, a_buf.at[pl.ds(q * slots, slots)], a_recv.at[0])

    def a_remote():
        mine = a_buf.at[pl.ds(q * slots, slots)]
        return pltpu.make_async_remote_copy(
            src_ref=blocks, dst_ref=mine, send_sem=a_send.at[0], recv_sem=a_recv.at[1],
            device_id=dev_core, device_id_type=MESH)

    def start(copies):
        for copy in copies:
            copy.start()

    def sent(copies):
        for copy in copies:
            copy.wait_send()

    def first(k, _):
        core_copy(k).start()
        return 0

    def first_local(k, _):
        own_copy(k).start()
        return 0

    def meta_copy():
        return pltpu.make_async_remote_copy(
            src_ref=meta, dst_ref=meta_in, send_sem=meta_sems.at[0], recv_sem=meta_sems.at[1],
            device_id=dev_core, device_id_type=MESH)

    lane = lax.broadcasted_iota(jnp.int32, (8, LANES), 1)

    def list_slots():
        number = lax.broadcasted_iota(jnp.int32, (1, slots), 1)
        key = jnp.where(number < live[...], rows[...] - i * 32, 32)
        place = lax.shift_right_logical(columns[...], 5) * 4 + q * 2 + (columns[...] & 1)
        meta[...] = jnp.full((8, LANES), 64, jnp.int32)

        @pl.when(q == 0)
        def _():
            meta[0:1, 0:slots] = key
            meta[1:2, 0:slots] = place

        @pl.when(q == 1)
        def _():
            meta[0:1, slots:2 * slots] = key
            meta[1:2, slots:2 * slots] = place

    def make_tables():
        meta_copy().wait()
        joint = jnp.where((lane >= q * slots) & (lane < (q + 1) * slots), meta[...], meta_in[...])
        square = (LANES, LANES)
        item = lax.broadcasted_iota(jnp.int32, square, 0)
        at = lax.broadcasted_iota(jnp.int32, square, 1)
        key_b = jnp.broadcast_to(joint[0:1], square)
        key_a = key_b.T
        place_a = jnp.broadcast_to(joint[1:2], square).T

        def count(mask):
            return jnp.sum(jnp.where(mask, 1, 0), axis=0, keepdims=True)

        def pick(mask, value):
            return jnp.sum(jnp.where(mask, value, 0), axis=0, keepdims=True)

        rank = count((key_a < key_b) | ((key_a == key_b) & (item < at)))
        rank_a = jnp.broadcast_to(rank, square).T
        hit = rank_a == at
        key_here = pick(hit, key_a)
        key_before = pick(rank_a + 1 == at, key_a)
        tab_v[...] = jnp.zeros((8, LANES), jnp.int32)
        tab_v[0:1] = pick(hit, item)
        tab_v[1:2] = pick(hit, place_a)
        tab_v[2:3] = jnp.where(count(key_a == at) > 0, count(key_a <= at), 0)
        keep_v[...] = jnp.broadcast_to(
            jnp.where((key_here == key_before) & (lane[0:1] > 0), 1.0, 0.0), (8, LANES))
        moves = [pltpu.make_async_copy(tab_v, tab, tab_sems.at[0]), pltpu.make_async_copy(keep_v, keep, tab_sems.at[1])]
        start(moves)
        for move in moves:
            move.wait()

    lax.fori_loop(0, chunks, first_local, 0)
    barrier = pltpu.get_barrier_semaphore()
    others = plane + line
    for dev in others:
        pl.semaphore_signal(barrier, inc=1, device_id=dev, device_id_type=MESH)
    a_local().start()
    q_buf[0] = jnp.zeros(q_buf.shape[1:], jnp.float32)
    ms[0] = jnp.zeros((8, LANES), jnp.float32)
    list_slots()
    pl.semaphore_wait(barrier, len(others))
    meta_copy().start()

    def stage_a(k):
        @pl.when(k >= TURNS)
        def _():
            sent([x_copy(k - TURNS)] + y_copies(k - TURNS))

        own_copy(k).wait()
        arrived(CORE, k, piece(k, i, (1 - q) * 2, 2), dev_core)
        start(y_copies(k))
        x_copy(k).start()

    def stage_b(k):
        @pl.when(k >= TURNS)
        def _():
            by_fork(k - TURNS, lambda forked: sent(yx_copies(k - TURNS, forked)))

        arrived(X, k, piece(k, xi), dev_x)
        by_fork(k, lambda forked: start(yx_copies(k, forked)))

    def stage_c(k):
        @pl.when(k >= TURNS)
        def _():
            sent(fwd_copies(k - TURNS) + fwdx_copies(k - TURNS))
            by_fork(k - TURNS, lambda forked: sent(fork_copies(k - TURNS, forked)))

        arrived(YPA, k, piece(k, ym), dev_ym)
        arrived(YMA, k, piece(k, yp), dev_yp)
        start(fwd_copies(k))

        def rest(forked):
            start(fork_copies(k, forked))
            arrived(YPB, k, piece(k, xym, 0, 4 - forked), dev_ym)
            arrived(YMB, k, piece(k, xyp, forked, 4 - forked), dev_yp)

        by_fork(k, rest)
        start(fwdx_copies(k))

    def partial(r):
        return q_buf[tab[2, r]]

    def compute(k):
        arrived(YPC, k, piece(k, y2, 0, 2), dev_ym)
        arrived(YMC, k, piece(k, y2, 2, 2), dev_yp)
        arrived(YPD, k, piece(k, xy2, 0, 2), dev_ym)
        arrived(YMD, k, piece(k, xy2, 2, 2), dev_yp)

        def by_x(forked):
            if forked:
                arrived(XF0, k, piece(k, xym, 4 - forked, forked), dev_x)
                arrived(XF1, k, piece(k, xyp, 0, forked), dev_x)

        by_fork(k, by_x)

        move = pltpu.make_async_copy(b_buf.at[k], b_cmp, cmp_sem.at[0])
        move.start()

        @pl.when(k == 0)
        def _():
            a_local().wait()
            pltpu.make_async_remote_copy(
                src_ref=blocks, dst_ref=a_buf.at[pl.ds((1 - q) * slots, slots)], send_sem=a_send.at[0],
                recv_sem=a_recv.at[1], device_id=dev_core, device_id_type=MESH).wait_recv()

        move.wait()

        def product(p, _):
            q_buf[p + 1] = keep[0, p] * q_buf[p] + jnp.dot(
                a_buf[tab[0, p]], b_cmp[tab[1, p]], preferred_element_type=jnp.float32)
            return 0

        lax.fori_loop(0, 2 * slots, product, 0, unroll=8)

        slot = lax.rem(k, 2)

        @pl.when(k >= 2)
        def _():
            x1_copy(k - 2).wait_send()
            for copy in m1_copies(k - 2) + m2a_copies(k - 2):
                copy.wait_send()

        def pack0(n, _):
            x1s[slot, n] = encode(partial((1 - xh) * 16 + n * 4 + 3))
            return 0

        lax.fori_loop(0, 4, pack0, 0)
        x1_copy(k).start()

        def pack1(n, _):
            m1s[slot, 0, n] = encode(partial(z2 * 4 + n))
            m1s[slot, 1, n] = encode(partial(16 + z2 * 4 + n))
            return 0

        lax.fori_loop(0, 3, pack1, 0)
        start(m1_copies(k))

        def pack2(n, _):
            m2as[slot, 0, n] = encode(partial(16 + zp * 4 + n))
            m2as[slot, 1, n] = encode(partial(zm * 4 + n))
            return 0

        lax.fori_loop(0, 3, pack2, 0)

        @pl.when(k == chunks - 1)
        def _():
            sent(m1_copies(k))

        start(m2a_copies(k))

        keep_slot = lax.rem(k, 3)

        def hold(n, _):
            t_buf[0, n] = partial(zp * 4 + n)
            t_buf[1, n] = partial(16 + zm * 4 + n)
            s_buf[keep_slot, 0, n] = partial(z * 4 + n)
            s_buf[keep_slot, 1, n] = partial(16 + z * 4 + n)
            return 0

        lax.fori_loop(0, 3, hold, 0)

        def hold_last(n, _):
            u_buf[n] = partial(xh * 16 + n * 4 + 3)
            return 0

        lax.fori_loop(0, 4, hold_last, 0)

    def relay(k):
        slot = lax.rem(k, 2)
        keep_slot = lax.rem(k, 3)

        @pl.when(k >= 2)
        def _():
            for copy in m2b_copies(k - 2) + ea_copies(k - 2):
                copy.wait_send()

        arrived(M1P, k, m1r.at[k, 0], dev_zm)
        arrived(M1M, k, m1r.at[k, 1], dev_zp)

        for n in range(SPLIT):
            for d in range(2):
                m2bs[slot, d, n] = encode(t_buf[d, n] + decode(m1r[k, d, n]))
            start(m2b_part(k, n))

        arrived(X1, k, x1r.at[k], dev_x2)

        def join(n, _):
            v_buf[keep_slot, n] = u_buf[n] + decode(x1r[k, n])
            return 0

        lax.fori_loop(0, 4, join, 0)
        eas[slot, 0, 0] = encode(v_buf[keep_slot, z2, LOW])
        eas[slot, 0, 1] = encode(v_buf[keep_slot, zp, HIGH])
        eas[slot, 1, 0] = encode(v_buf[keep_slot, z2, HIGH])
        eas[slot, 1, 1] = encode(v_buf[keep_slot, zm, LOW])
        start(ea_copies(k))

    def collect(k):
        slot = lax.rem(k, 2)
        keep_slot = lax.rem(k, 3)

        @pl.when(k >= 2)
        def _():
            sent(mx_copies(k - 2) + eb_copies(k - 2))

        arrived(M2AP, k, m2ar.at[k, 0], dev_zm)
        arrived(M2AM, k, m2ar.at[k, 1], dev_zp)

        def total(h, n):
            return s_buf[keep_slot, h, n] + (decode(m2br[k, h, n]) + decode(m2ar[k, 1 - h, n]))

        for n in range(SPLIT):
            arrived(M2BP + 3 * n, k, m2br.at[k, 0, n], dev_zm)
            arrived(M2BM + 3 * n, k, m2br.at[k, 1, n], dev_zp)
            mxs[slot, n] = encode(total(1 - xh, n))
            mx_part(k, n).start()

        arrived(EAP, k, ear.at[k, 0], dev_zm)
        arrived(EAM, k, ear.at[k, 1], dev_zp)
        ebs[slot, 0] = encode(v_buf[keep_slot, zp, LOW] + decode(ear[k, 0, 0]))
        ebs[slot, 1] = encode(v_buf[keep_slot, zm, HIGH] + decode(ear[k, 1, 0]))
        start(eb_copies(k))

        def hold(n, _):
            s_buf[keep_slot, xh, n] = total(xh, n)
            return 0

        lax.fori_loop(0, 3, hold, 0)

    lane_row = lax.broadcasted_iota(jnp.int32, (8, LANES), 0)

    def finish(k):
        slot = lax.rem(k, 2)
        keep_slot = lax.rem(k, 3)

        @pl.when(k >= 2)
        def _():
            outc_copy(k - 2).wait_send()
            outl_copy(k - 2).wait()

        arrived(EBP, k, ebr.at[k, 0], dev_zm)
        arrived(EBM, k, ebr.at[k, 1], dev_zp)
        low = v_buf[keep_slot, z, LOW] + (decode(ebr[k, 0]) + decode(ear[k, 1, 1]))
        high = v_buf[keep_slot, z, HIGH] + (decode(ebr[k, 1]) + decode(ear[k, 0, 1]))
        fin[slot, 3, LOW] = low
        fin[slot, 3, HIGH] = high
        acc = jnp.sum((low * low + high * high).reshape(-1, 8, LANES), axis=0)

        for n in range(SPLIT):
            arrived(MX + 3 * n, k, mxr.at[k, n], dev_x2)
            value = s_buf[keep_slot, xh, n] + decode(mxr[k, n])
            fin[slot, n] = value
            acc = acc + jnp.sum((value * value).reshape(-1, 8, LANES), axis=0)

        outc_copy(k).start()
        outl_copy(k).start()
        ms[0] = jnp.where(lane_row == k, jnp.sum(acc, axis=0, keepdims=True), ms[0])

    core_copy(0).start()
    core_copy(1).start()
    a_remote().start()
    lax.fori_loop(2, chunks, first, 0)
    stage_a(0)
    stage_b(0)
    stage_a(1)
    make_tables()

    def step(t, _):
        @pl.when(t < chunks)
        def _():
            stage_c(t)

        @pl.when(t + 1 < chunks)
        def _():
            stage_b(t + 1)

        @pl.when(t + 2 < chunks)
        def _():
            stage_a(t + 2)

        @pl.when((t >= 1) & (t - 1 < chunks))
        def _():
            relay(t - 1)

        @pl.when((t >= 2) & (t - 2 < chunks))
        def _():
            collect(t - 2)

        @pl.when(t >= 3)
        def _():
            finish(t - 3)

        @pl.when(t < chunks)
        def _():
            compute(t)

        return 0

    lax.fori_loop(0, chunks + 3, step, 0)

    copies = [pltpu.make_async_remote_copy(
        src_ref=ms.at[0], dst_ref=mr_plane.at[n], send_sem=mass_send.at[n], recv_sem=mass_recv.at[n],
        device_id=dev, device_id_type=MESH) for n, dev in enumerate(plane)]
    start(copies)

    a_remote().wait_send()

    def drain(k, _):
        core_copy(k).wait_send()
        arrived(OUTC, k, e_out.at[:, :, cols(1 - q, k)], dev_core)
        return 0

    lax.fori_loop(0, chunks, drain, 0)

    def drain_pieces(k, _):
        sent([x_copy(k)] + y_copies(k) + fwd_copies(k) + fwdx_copies(k))
        by_fork(k, lambda forked: sent(yx_copies(k, forked) + fork_copies(k, forked)))
        return 0

    lax.fori_loop(chunks - TURNS, chunks, drain_pieces, 0)

    sent(m1_copies(chunks - 2))

    def drain_last(k, _):
        for copy in m2a_copies(k) + m2b_copies(k) + ea_copies(k) + eb_copies(k):
            copy.wait_send()
        x1_copy(k).wait_send()
        sent(mx_copies(k))
        outc_copy(k).wait_send()
        outl_copy(k).wait()
        return 0

    lax.fori_loop(chunks - 2, chunks, drain_last, 0)

    for copy in copies:
        copy.wait()
    ms[1] = ms[0] + jnp.sum(mr_plane[...], axis=0)
    copies = [pltpu.make_async_remote_copy(
        src_ref=ms.at[1], dst_ref=mr_line.at[n], send_sem=mass_send.at[15 + n], recv_sem=mass_recv.at[15 + n],
        device_id=dev, device_id_type=MESH) for n, dev in enumerate(line)]
    start(copies)
    for copy in copies:
        copy.wait()
    mass_out[q] = ms[1] + jnp.sum(mr_line[0:3], axis=0)
    mass_out[1 - q] = jnp.sum(mr_line[3:7], axis=0)


def body(blocks, block_rows, block_cols, live_count, slab):
    slots, bs = blocks.shape[2], blocks.shape[3]
    depth, width = slab.shape
    chunks = width // 2 // LANES
    f32, bf16 = jnp.float32, jnp.bfloat16
    tile, half = (bs, LANES), (bs // 2, LANES)
    vm = pltpu.VMEM
    e, mass = pl.pallas_call(
        functools.partial(kernel, chunks, slots),
        out_shape=(jax.ShapeDtypeStruct((2, bs, width), f32), jax.ShapeDtypeStruct((2, chunks, LANES), f32)),
        in_specs=[pl.BlockSpec(memory_space=pltpu.VMEM), pl.BlockSpec(memory_space=pltpu.VMEM),
                  pl.BlockSpec(memory_space=pltpu.VMEM),
                  pl.BlockSpec(memory_space=pl.ANY), pl.BlockSpec(memory_space=pl.ANY)],
        out_specs=(pl.BlockSpec(memory_space=pl.ANY), pl.BlockSpec(memory_space=pltpu.VMEM)),
        scratch_shapes=[
            vm((2 * slots, bs, bs), bf16),
            vm((chunks, 32) + tile, bf16),
            vm((32,) + tile, bf16),
            vm((2 * slots + 1,) + tile, f32),
            vm((3, 2, 3) + tile, f32),
            vm((2, 3) + tile, f32),
            vm((2, 2, 3) + tile, bf16), vm((chunks, 2, 3) + tile, bf16),
            vm((2, 2, 3) + tile, bf16), vm((chunks, 2, 3) + tile, bf16),
            vm((2, 2, 3) + tile, bf16), vm((chunks, 2, 3) + tile, bf16),
            vm((2, 3) + tile, bf16), vm((chunks, 3) + tile, bf16),
            vm((2, 4) + tile, bf16), vm((chunks, 4) + tile, bf16),
            vm((2, 2, 2) + half, bf16), vm((chunks, 2, 2) + half, bf16),
            vm((2, 2) + half, bf16), vm((chunks, 2) + half, bf16),
            vm((4,) + tile, f32), vm((3, 4) + tile, f32),
            vm((2, 4) + tile, f32),
            vm((2, chunks, LANES), f32), vm((15, chunks, LANES), f32), vm((7, chunks, LANES), f32),
            vm((8, LANES), jnp.int32), vm((8, LANES), jnp.int32), vm((8, LANES), jnp.int32), vm((8, LANES), f32),
            pltpu.SMEM((8, LANES), jnp.int32), pltpu.SMEM((8, LANES), f32),
            pltpu.SemaphoreType.DMA((2, chunks)), pltpu.SemaphoreType.DMA((WIDE, chunks)),
            pltpu.SemaphoreType.DMA((KINDS - WIDE, TURNS)), pltpu.SemaphoreType.DMA((KINDS - WIDE, TURNS)),
            pltpu.SemaphoreType.DMA((1,)), pltpu.SemaphoreType.DMA((2,)),
            pltpu.SemaphoreType.DMA((22,)), pltpu.SemaphoreType.DMA((22,)),
            pltpu.SemaphoreType.DMA((1,)), pltpu.SemaphoreType.DMA((2,)), pltpu.SemaphoreType.DMA((2,)),
        ],
        compiler_params=pltpu.CompilerParams(
            collective_id=0, has_side_effects=True, vmem_limit_bytes=58 * 1024 * 1024),
        cost_estimate=pl.CostEstimate(
            flops=2 * 2 * slots * bs * bs * width // 2, bytes_accessed=16 * 2**20, transcendentals=0),
    )(block_rows.reshape(1, slots), block_cols.reshape(1, slots), live_count, blocks.reshape(slots, bs, bs), slab.reshape(2, bs, width))
    scale = depth * 128 / mass.reshape(1, 1, width)
    return (e * e * scale).reshape(depth, width)


def solution(mesh):
    placed = (
        P("row", "col", None, None, None),
        P("row", "col", None),
        P("row", "col", None),
        P("row", "col"),
        P(("row", "col"), None),
    )
    return jax.shard_map(
        body, mesh=mesh, in_specs=placed, out_specs=P(("row", "col"), None), check_vma=False
    )
```

```python
import functools

import jax
import jax.numpy as jnp
from jax import lax
from jax.experimental import pallas as pl
from jax.experimental.pallas import tpu as pltpu
from jax.sharding import PartitionSpec as P

MESH = pl.DeviceIdType.MESH
LOW, HIGH = pl.ds(0, 128), pl.ds(128, 128)

LANES = 128
FORK_TWO, FORK_ONE = 2, 4
MID, POWER, FLOOR = 6.0, 26.0, 117.0
LN2 = 0.6931471805599453

(OWN, CORE, OUTC, OUTL,
 X, YPA, YMA, YPB, YMB, YPC, YMC, YPD, YMD, XF0, XF1,
 M1P, M1M, M2AP, M2AM, X1, EAP, EAM, EBP, EBM, M2BP, M2BM, MX) = range(27)
SPLIT = 3
WIDE, KINDS, TURNS = 4, 27 + 3 * (SPLIT - 1), 3


def encode(x):
    u = jnp.log(x) * (1.0 / LN2) - MID
    y = jnp.exp2(jnp.abs(u) * POWER - FLOOR)
    return jnp.where(x > 0.0, jnp.where(u < 0.0, -y, y), 0.0).astype(jnp.bfloat16)


def decode(y):
    y = y.astype(jnp.float32)
    u = jnp.log(jnp.abs(y)) * (1.0 / (POWER * LN2)) + FLOOR / POWER
    return jnp.exp2(jnp.where(y < 0.0, -u, u) + MID)


def kernel(chunks, slots, rows, columns, live, blocks, slab, e_out, mass_out,
           a_buf, b_buf, b_cmp, q_buf, s_buf, t_buf,
           m1s, m1r, m2as, m2ar, m2bs, m2br, mxs, mxr, x1s, x1r, eas, ear, ebs, ebr, u_buf, v_buf,
           fin, ms, mr_plane, mr_line,
           meta, meta_in, tab_v, keep_v, tab, keep,
           wide_send, wide_recv, send, recv, a_send, a_recv, mass_send, mass_recv, cmp_sem, meta_sems, tab_sems):
    i = lax.axis_index("row")
    j = lax.axis_index("col")
    y = lax.rem(i, 4)
    yb = i - y
    q = lax.rem(j, 2)
    z = lax.rem(j // 2, 4)
    xh = j // 8
    zb = xh * 8 + q

    def row_y(d):
        return yb + lax.rem(y + d, 4)

    def col_z(d):
        return zb + 2 * lax.rem(z + d, 4)

    def flip(r):
        return lax.rem(r + 4, 8)

    xi = flip(i)
    yp, y2, ym = row_y(1), row_y(2), row_y(3)
    xyp, xy2, xym = flip(yp), flip(y2), flip(ym)
    jc = j + 1 - 2 * q
    jx = lax.rem(j + 8, 16)
    zp, z2, zm = lax.rem(z + 1, 4), lax.rem(z + 2, 4), lax.rem(z + 3, 4)

    dev_core = (i, jc)
    dev_x = (xi, j)
    dev_x2 = (i, jx)
    dev_yp, dev_ym = (yp, j), (ym, j)
    dev_zp, dev_zm = (i, col_z(1)), (i, col_z(3))
    plane = [(lax.rem(yb + 4 * fx, 8) + lax.rem(y + d, 4), lax.rem(j + 8 * fh, 16))
             for fx in range(2) for d in range(4) for fh in range(2)][1:]
    line = [(i, col_z(d)) for d in (1, 2, 3)] + [(i, col_z(d) + 1 - 2 * q) for d in range(4)]

    def cols(half, k):
        return pl.ds(pl.multiple_of(half * (chunks * LANES) + k * LANES, LANES), LANES)

    def remote(kind, k, src, dst, dev):
        if kind < WIDE:
            sems = wide_send.at[kind - CORE, k], wide_recv.at[kind, k]
        else:
            sems = send.at[kind - WIDE, lax.rem(k, TURNS)], recv.at[kind - WIDE, lax.rem(k, TURNS)]
        return pltpu.make_async_remote_copy(
            src_ref=src, dst_ref=dst, send_sem=sems[0], recv_sem=sems[1], device_id=dev, device_id_type=MESH)

    def arrived(kind, k, ref, dev):
        remote(kind, k, ref, ref, dev).wait_recv()

    def piece(k, r, first=0, count=4):
        return b_buf.at[k, pl.ds(r * 4 + first, count)]

    def own_copy(k):
        return pltpu.make_async_copy(slab.at[:, :, cols(q, k)], piece(k, i, q * 2, 2), wide_recv.at[OWN, k])

    def core_copy(k):
        return remote(CORE, k, slab.at[:, :, cols(1 - q, k)], piece(k, i, q * 2, 2), dev_core)

    def piece_copy(kind, k, r, dev, first=0, count=4):
        return remote(kind, k, piece(k, r, first, count), piece(k, r, first, count), dev)

    def x_copy(k):
        return piece_copy(X, k, i, dev_x)

    def y_copies(k):
        return [piece_copy(YPA, k, i, dev_yp), piece_copy(YMA, k, i, dev_ym)]

    def yx_copies(k, forked):
        return [piece_copy(YPB, k, xi, dev_yp, 0, 4 - forked), piece_copy(YMB, k, xi, dev_ym, forked, 4 - forked)]

    def fork_copies(k, forked):
        if not forked:
            return []
        return [piece_copy(XF0, k, ym, dev_x, 4 - forked, forked), piece_copy(XF1, k, yp, dev_x, 0, forked)]

    def by_fork(k, act):
        @pl.when(k < FORK_TWO)
        def _():
            act(2)

        @pl.when((k >= FORK_TWO) & (k < FORK_ONE))
        def _():
            act(1)

        @pl.when(k >= FORK_ONE)
        def _():
            act(0)

    def fwd_copies(k):
        return [piece_copy(YPC, k, ym, dev_yp, 0, 2), piece_copy(YMC, k, yp, dev_ym, 2, 2)]

    def fwdx_copies(k):
        return [piece_copy(YPD, k, xym, dev_yp, 0, 2), piece_copy(YMD, k, xyp, dev_ym, 2, 2)]

    def pair_copies(kp, k, src, dst):
        slot = lax.rem(k, 2)
        return [remote(kp, k, src.at[slot, 0], dst.at[k, 0], dev_zp),
                remote(kp + 1, k, src.at[slot, 1], dst.at[k, 1], dev_zm)]

    def m1_copies(k):
        return pair_copies(M1P, k, m1s, m1r)

    def m2a_copies(k):
        return pair_copies(M2AP, k, m2as, m2ar)

    def m2b_part(k, n):
        slot = lax.rem(k, 2)
        return [remote(M2BP + 3 * n, k, m2bs.at[slot, 0, n], m2br.at[k, 0, n], dev_zp),
                remote(M2BM + 3 * n, k, m2bs.at[slot, 1, n], m2br.at[k, 1, n], dev_zm)]

    def m2b_copies(k):
        return m2b_part(k, 0) + m2b_part(k, 1) + m2b_part(k, 2)

    def x1_copy(k):
        return remote(X1, k, x1s.at[lax.rem(k, 2)], x1r.at[k], dev_x2)

    def ea_copies(k):
        return pair_copies(EAP, k, eas, ear)

    def eb_copies(k):
        return pair_copies(EBP, k, ebs, ebr)

    def mx_part(k, n):
        return remote(MX + 3 * n, k, mxs.at[lax.rem(k, 2), n], mxr.at[k, n], dev_x2)

    def mx_copies(k):
        return [mx_part(k, n) for n in range(SPLIT)]

    def outc_copy(k):
        return remote(OUTC, k, fin.at[lax.rem(k, 2), pl.ds((1 - q) * 2, 2)], e_out.at[:, :, cols(q, k)], dev_core)

    def outl_copy(k):
        return pltpu.make_async_copy(fin.at[lax.rem(k, 2), pl.ds(q * 2, 2)], e_out.at[:, :, cols(q, k)], wide_recv.at[OUTL, k])

    def a_local():
        return pltpu.make_async_copy(blocks, a_buf.at[pl.ds(q * slots, slots)], a_recv.at[0])

    def a_remote():
        mine = a_buf.at[pl.ds(q * slots, slots)]
        return pltpu.make_async_remote_copy(
            src_ref=blocks, dst_ref=mine, send_sem=a_send.at[0], recv_sem=a_recv.at[1],
            device_id=dev_core, device_id_type=MESH)

    def start(copies):
        for copy in copies:
            copy.start()

    def sent(copies):
        for copy in copies:
            copy.wait_send()

    def first(k, _):
        core_copy(k).start()
        return 0

    def first_local(k, _):
        own_copy(k).start()
        return 0

    def meta_copy():
        return pltpu.make_async_remote_copy(
            src_ref=meta, dst_ref=meta_in, send_sem=meta_sems.at[0], recv_sem=meta_sems.at[1],
            device_id=dev_core, device_id_type=MESH)

    lane = lax.broadcasted_iota(jnp.int32, (8, LANES), 1)

    def list_slots():
        number = lax.broadcasted_iota(jnp.int32, (1, slots), 1)
        key = jnp.where(number < live[...], rows[...] - i * 32, 32)
        place = lax.shift_right_logical(columns[...], 5) * 4 + q * 2 + (columns[...] & 1)
        meta[...] = jnp.full((8, LANES), 64, jnp.int32)

        @pl.when(q == 0)
        def _():
            meta[0:1, 0:slots] = key
            meta[1:2, 0:slots] = place

        @pl.when(q == 1)
        def _():
            meta[0:1, slots:2 * slots] = key
            meta[1:2, slots:2 * slots] = place

    def make_tables():
        meta_copy().wait()
        joint = jnp.where((lane >= q * slots) & (lane < (q + 1) * slots), meta[...], meta_in[...])
        square = (LANES, LANES)
        item = lax.broadcasted_iota(jnp.int32, square, 0)
        at = lax.broadcasted_iota(jnp.int32, square, 1)
        key_b = jnp.broadcast_to(joint[0:1], square)
        key_a = key_b.T
        place_a = jnp.broadcast_to(joint[1:2], square).T

        def count(mask):
            return jnp.sum(jnp.where(mask, 1, 0), axis=0, keepdims=True)

        def pick(mask, value):
            return jnp.sum(jnp.where(mask, value, 0), axis=0, keepdims=True)

        rank = count((key_a < key_b) | ((key_a == key_b) & (item < at)))
        rank_a = jnp.broadcast_to(rank, square).T
        hit = rank_a == at
        key_here = pick(hit, key_a)
        key_before = pick(rank_a + 1 == at, key_a)
        tab_v[...] = jnp.zeros((8, LANES), jnp.int32)
        tab_v[0:1] = pick(hit, item)
        tab_v[1:2] = pick(hit, place_a)
        tab_v[2:3] = jnp.where(count(key_a == at) > 0, count(key_a <= at), 0)
        keep_v[...] = jnp.broadcast_to(
            jnp.where((key_here == key_before) & (lane[0:1] > 0), 1.0, 0.0), (8, LANES))
        moves = [pltpu.make_async_copy(tab_v, tab, tab_sems.at[0]), pltpu.make_async_copy(keep_v, keep, tab_sems.at[1])]
        start(moves)
        for move in moves:
            move.wait()

    lax.fori_loop(0, chunks, first_local, 0)
    barrier = pltpu.get_barrier_semaphore()
    others = plane + line
    for dev in others:
        pl.semaphore_signal(barrier, inc=1, device_id=dev, device_id_type=MESH)
    a_local().start()
    q_buf[0] = jnp.zeros(q_buf.shape[1:], jnp.float32)
    ms[0] = jnp.zeros((8, LANES), jnp.float32)
    list_slots()
    pl.semaphore_wait(barrier, len(others))
    meta_copy().start()

    def stage_a(k):
        @pl.when(k >= TURNS)
        def _():
            sent([x_copy(k - TURNS)] + y_copies(k - TURNS))

        own_copy(k).wait()
        arrived(CORE, k, piece(k, i, (1 - q) * 2, 2), dev_core)
        start(y_copies(k))
        x_copy(k).start()

    def stage_b(k):
        @pl.when(k >= TURNS)
        def _():
            by_fork(k - TURNS, lambda forked: sent(yx_copies(k - TURNS, forked)))

        arrived(X, k, piece(k, xi), dev_x)
        by_fork(k, lambda forked: start(yx_copies(k, forked)))

    def stage_c(k):
        @pl.when(k >= TURNS)
        def _():
            sent(fwd_copies(k - TURNS) + fwdx_copies(k - TURNS))
            by_fork(k - TURNS, lambda forked: sent(fork_copies(k - TURNS, forked)))

        arrived(YPA, k, piece(k, ym), dev_ym)
        arrived(YMA, k, piece(k, yp), dev_yp)
        start(fwd_copies(k))

        def rest(forked):
            start(fork_copies(k, forked))
            arrived(YPB, k, piece(k, xym, 0, 4 - forked), dev_ym)
            arrived(YMB, k, piece(k, xyp, forked, 4 - forked), dev_yp)

        by_fork(k, rest)
        start(fwdx_copies(k))

    def partial(r):
        return q_buf[tab[2, r]]

    def compute(k):
        arrived(YPC, k, piece(k, y2, 0, 2), dev_ym)
        arrived(YMC, k, piece(k, y2, 2, 2), dev_yp)
        arrived(YPD, k, piece(k, xy2, 0, 2), dev_ym)
        arrived(YMD, k, piece(k, xy2, 2, 2), dev_yp)

        def by_x(forked):
            if forked:
                arrived(XF0, k, piece(k, xym, 4 - forked, forked), dev_x)
                arrived(XF1, k, piece(k, xyp, 0, forked), dev_x)

        by_fork(k, by_x)

        move = pltpu.make_async_copy(b_buf.at[k], b_cmp, cmp_sem.at[0])
        move.start()

        @pl.when(k == 0)
        def _():
            a_local().wait()
            pltpu.make_async_remote_copy(
                src_ref=blocks, dst_ref=a_buf.at[pl.ds((1 - q) * slots, slots)], send_sem=a_send.at[0],
                recv_sem=a_recv.at[1], device_id=dev_core, device_id_type=MESH).wait_recv()

        move.wait()

        def product(p, _):
            q_buf[p + 1] = keep[0, p] * q_buf[p] + jnp.dot(
                a_buf[tab[0, p]], b_cmp[tab[1, p]], preferred_element_type=jnp.float32)
            return 0

        lax.fori_loop(0, 2 * slots, product, 0, unroll=16)

        slot = lax.rem(k, 2)

        @pl.when(k >= 2)
        def _():
            x1_copy(k - 2).wait_send()
            for copy in m1_copies(k - 2) + m2a_copies(k - 2):
                copy.wait_send()

        def pack0(n, _):
            x1s[slot, n] = encode(partial((1 - xh) * 16 + n * 4 + 3))
            return 0

        lax.fori_loop(0, 4, pack0, 0)
        x1_copy(k).start()

        def pack1(n, _):
            m1s[slot, 0, n] = encode(partial(z2 * 4 + n))
            m1s[slot, 1, n] = encode(partial(16 + z2 * 4 + n))
            return 0

        lax.fori_loop(0, 3, pack1, 0)
        start(m1_copies(k))

        def pack2(n, _):
            m2as[slot, 0, n] = encode(partial(16 + zp * 4 + n))
            m2as[slot, 1, n] = encode(partial(zm * 4 + n))
            return 0

        lax.fori_loop(0, 3, pack2, 0)

        start(m2a_copies(k))

        keep_slot = lax.rem(k, 3)

        def hold(n, _):
            t_buf[0, n] = partial(zp * 4 + n)
            t_buf[1, n] = partial(16 + zm * 4 + n)
            s_buf[keep_slot, 0, n] = partial(z * 4 + n)
            s_buf[keep_slot, 1, n] = partial(16 + z * 4 + n)
            return 0

        lax.fori_loop(0, 3, hold, 0)

        def hold_last(n, _):
            u_buf[n] = partial(xh * 16 + n * 4 + 3)
            return 0

        lax.fori_loop(0, 4, hold_last, 0)

    def relay(k):
        slot = lax.rem(k, 2)
        keep_slot = lax.rem(k, 3)

        @pl.when(k >= 2)
        def _():
            for copy in m2b_copies(k - 2) + ea_copies(k - 2):
                copy.wait_send()

        arrived(M1P, k, m1r.at[k, 0], dev_zm)
        arrived(M1M, k, m1r.at[k, 1], dev_zp)

        for n in range(SPLIT):
            for d in range(2):
                m2bs[slot, d, n] = encode(t_buf[d, n] + decode(m1r[k, d, n]))
            start(m2b_part(k, n))

        arrived(X1, k, x1r.at[k], dev_x2)

        def join(n, _):
            v_buf[keep_slot, n] = u_buf[n] + decode(x1r[k, n])
            return 0

        lax.fori_loop(0, 4, join, 0)
        eas[slot, 0, 0] = encode(v_buf[keep_slot, z2, LOW])
        eas[slot, 0, 1] = encode(v_buf[keep_slot, zp, HIGH])
        eas[slot, 1, 0] = encode(v_buf[keep_slot, z2, HIGH])
        eas[slot, 1, 1] = encode(v_buf[keep_slot, zm, LOW])
        start(ea_copies(k))

    def collect(k):
        slot = lax.rem(k, 2)
        keep_slot = lax.rem(k, 3)

        @pl.when(k >= 2)
        def _():
            sent(mx_copies(k - 2) + eb_copies(k - 2))

        arrived(M2AP, k, m2ar.at[k, 0], dev_zm)
        arrived(M2AM, k, m2ar.at[k, 1], dev_zp)

        def total(h, n):
            return s_buf[keep_slot, h, n] + (decode(m2br[k, h, n]) + decode(m2ar[k, 1 - h, n]))

        for n in range(SPLIT):
            arrived(M2BP + 3 * n, k, m2br.at[k, 0, n], dev_zm)
            arrived(M2BM + 3 * n, k, m2br.at[k, 1, n], dev_zp)
            mxs[slot, n] = encode(total(1 - xh, n))
            mx_part(k, n).start()

        arrived(EAP, k, ear.at[k, 0], dev_zm)
        arrived(EAM, k, ear.at[k, 1], dev_zp)
        ebs[slot, 0] = encode(v_buf[keep_slot, zp, LOW] + decode(ear[k, 0, 0]))
        ebs[slot, 1] = encode(v_buf[keep_slot, zm, HIGH] + decode(ear[k, 1, 0]))
        start(eb_copies(k))

        def hold(n, _):
            s_buf[keep_slot, xh, n] = total(xh, n)
            return 0

        lax.fori_loop(0, 3, hold, 0)

    lane_row = lax.broadcasted_iota(jnp.int32, (8, LANES), 0)

    def finish(k):
        slot = lax.rem(k, 2)
        keep_slot = lax.rem(k, 3)

        @pl.when(k >= 2)
        def _():
            outc_copy(k - 2).wait_send()
            outl_copy(k - 2).wait()

        arrived(EBP, k, ebr.at[k, 0], dev_zm)
        arrived(EBM, k, ebr.at[k, 1], dev_zp)
        low = v_buf[keep_slot, z, LOW] + (decode(ebr[k, 0]) + decode(ear[k, 1, 1]))
        high = v_buf[keep_slot, z, HIGH] + (decode(ebr[k, 1]) + decode(ear[k, 0, 1]))
        fin[slot, 3, LOW] = low
        fin[slot, 3, HIGH] = high
        acc = jnp.sum((low * low + high * high).reshape(-1, 8, LANES), axis=0)

        for n in range(SPLIT):
            arrived(MX + 3 * n, k, mxr.at[k, n], dev_x2)
            value = s_buf[keep_slot, xh, n] + decode(mxr[k, n])
            fin[slot, n] = value
            acc = acc + jnp.sum((value * value).reshape(-1, 8, LANES), axis=0)

        outc_copy(k).start()
        outl_copy(k).start()
        ms[0] = jnp.where(lane_row == k, jnp.sum(acc, axis=0, keepdims=True), ms[0])

    core_copy(0).start()
    core_copy(1).start()
    a_remote().start()
    lax.fori_loop(2, chunks, first, 0)
    stage_a(0)
    stage_b(0)
    stage_a(1)
    make_tables()

    def step(t, _):
        @pl.when(t < chunks)
        def _():
            stage_c(t)

        @pl.when(t + 1 < chunks)
        def _():
            stage_b(t + 1)

        @pl.when(t + 2 < chunks)
        def _():
            stage_a(t + 2)

        @pl.when((t >= 1) & (t - 1 < chunks))
        def _():
            relay(t - 1)

        @pl.when((t >= 2) & (t - 2 < chunks))
        def _():
            collect(t - 2)

        @pl.when(t >= 3)
        def _():
            finish(t - 3)

        @pl.when(t < chunks)
        def _():
            compute(t)

        return 0

    lax.fori_loop(0, chunks + 3, step, 0)

    copies = [pltpu.make_async_remote_copy(
        src_ref=ms.at[0], dst_ref=mr_plane.at[n], send_sem=mass_send.at[n], recv_sem=mass_recv.at[n],
        device_id=dev, device_id_type=MESH) for n, dev in enumerate(plane)]
    start(copies)

    a_remote().wait_send()

    def drain(k, _):
        core_copy(k).wait_send()
        arrived(OUTC, k, e_out.at[:, :, cols(1 - q, k)], dev_core)
        return 0

    lax.fori_loop(0, chunks, drain, 0)

    def drain_pieces(k, _):
        sent([x_copy(k)] + y_copies(k) + fwd_copies(k) + fwdx_copies(k))
        by_fork(k, lambda forked: sent(yx_copies(k, forked) + fork_copies(k, forked)))
        return 0

    lax.fori_loop(chunks - TURNS, chunks, drain_pieces, 0)

    sent(m1_copies(chunks - 2))
    sent(m1_copies(chunks - 1))

    def drain_last(k, _):
        for copy in m2a_copies(k) + m2b_copies(k) + ea_copies(k) + eb_copies(k):
            copy.wait_send()
        x1_copy(k).wait_send()
        sent(mx_copies(k))
        outc_copy(k).wait_send()
        outl_copy(k).wait()
        return 0

    lax.fori_loop(chunks - 2, chunks, drain_last, 0)

    for copy in copies:
        copy.wait()
    ms[1] = ms[0] + jnp.sum(mr_plane[...], axis=0)
    copies = [pltpu.make_async_remote_copy(
        src_ref=ms.at[1], dst_ref=mr_line.at[n], send_sem=mass_send.at[15 + n], recv_sem=mass_recv.at[15 + n],
        device_id=dev, device_id_type=MESH) for n, dev in enumerate(line)]
    start(copies)
    for copy in copies:
        copy.wait()
    mass_out[q] = ms[1] + jnp.sum(mr_line[0:3], axis=0)
    mass_out[1 - q] = jnp.sum(mr_line[3:7], axis=0)


def body(blocks, block_rows, block_cols, live_count, slab):
    slots, bs = blocks.shape[2], blocks.shape[3]
    depth, width = slab.shape
    chunks = width // 2 // LANES
    f32, bf16 = jnp.float32, jnp.bfloat16
    tile, half = (bs, LANES), (bs // 2, LANES)
    vm = pltpu.VMEM
    e, mass = pl.pallas_call(
        functools.partial(kernel, chunks, slots),
        out_shape=(jax.ShapeDtypeStruct((2, bs, width), f32), jax.ShapeDtypeStruct((2, chunks, LANES), f32)),
        in_specs=[pl.BlockSpec(memory_space=pltpu.VMEM), pl.BlockSpec(memory_space=pltpu.VMEM),
                  pl.BlockSpec(memory_space=pltpu.VMEM),
                  pl.BlockSpec(memory_space=pl.ANY), pl.BlockSpec(memory_space=pl.ANY)],
        out_specs=(pl.BlockSpec(memory_space=pl.ANY), pl.BlockSpec(memory_space=pltpu.VMEM)),
        scratch_shapes=[
            vm((2 * slots, bs, bs), bf16),
            vm((chunks, 32) + tile, bf16),
            vm((32,) + tile, bf16),
            vm((2 * slots + 1,) + tile, f32),
            vm((3, 2, 3) + tile, f32),
            vm((2, 3) + tile, f32),
            vm((2, 2, 3) + tile, bf16), vm((chunks, 2, 3) + tile, bf16),
            vm((2, 2, 3) + tile, bf16), vm((chunks, 2, 3) + tile, bf16),
            vm((2, 2, 3) + tile, bf16), vm((chunks, 2, 3) + tile, bf16),
            vm((2, 3) + tile, bf16), vm((chunks, 3) + tile, bf16),
            vm((2, 4) + tile, bf16), vm((chunks, 4) + tile, bf16),
            vm((2, 2, 2) + half, bf16), vm((chunks, 2, 2) + half, bf16),
            vm((2, 2) + half, bf16), vm((chunks, 2) + half, bf16),
            vm((4,) + tile, f32), vm((3, 4) + tile, f32),
            vm((2, 4) + tile, f32),
            vm((2, chunks, LANES), f32), vm((15, chunks, LANES), f32), vm((7, chunks, LANES), f32),
            vm((8, LANES), jnp.int32), vm((8, LANES), jnp.int32), vm((8, LANES), jnp.int32), vm((8, LANES), f32),
            pltpu.SMEM((8, LANES), jnp.int32), pltpu.SMEM((8, LANES), f32),
            pltpu.SemaphoreType.DMA((2, chunks)), pltpu.SemaphoreType.DMA((WIDE, chunks)),
            pltpu.SemaphoreType.DMA((KINDS - WIDE, TURNS)), pltpu.SemaphoreType.DMA((KINDS - WIDE, TURNS)),
            pltpu.SemaphoreType.DMA((1,)), pltpu.SemaphoreType.DMA((2,)),
            pltpu.SemaphoreType.DMA((22,)), pltpu.SemaphoreType.DMA((22,)),
            pltpu.SemaphoreType.DMA((1,)), pltpu.SemaphoreType.DMA((2,)), pltpu.SemaphoreType.DMA((2,)),
        ],
        compiler_params=pltpu.CompilerParams(
            collective_id=0, has_side_effects=True, vmem_limit_bytes=58 * 1024 * 1024),
        cost_estimate=pl.CostEstimate(
            flops=2 * 2 * slots * bs * bs * width // 2, bytes_accessed=16 * 2**20, transcendentals=0),
    )(block_rows.reshape(1, slots), block_cols.reshape(1, slots), live_count, blocks.reshape(slots, bs, bs), slab.reshape(2, bs, width))
    scale = depth * 128 / mass.reshape(1, 1, width)
    return (e * e * scale).reshape(depth, width)


def solution(mesh):
    placed = (
        P("row", "col", None, None, None),
        P("row", "col", None),
        P("row", "col", None),
        P("row", "col"),
        P(("row", "col"), None),
    )
    return jax.shard_map(
        body, mesh=mesh, in_specs=placed, out_specs=P(("row", "col"), None), check_vma=False
    )
```
